32 devices in a mesh: row: 8 (over y, x, core), col: 4 (over z).
Axes of the slice: x: 2, y: 2, z: 4, core: 2. Of those that a mesh axis runs over, the one named last changes fastest.
Arguments:
- enc_out: bfloat16 [2048, 4096], P(('row', 'col')), may hold values from -6 to 6
- keep: int32 [32, 64], P('row'), may hold values from 0 to 255, as said below
- pos_ids: int32 [32, 256], P('row'), may hold values from 0 to 1023
- mask_token: bfloat16 [4096], P('col'), may hold values from -5 to 5
- pos_table: bfloat16 [1024, 4096], P(None, 'col'), may hold values from -4 to 4
- gain: bfloat16 [4096], P('col'), may hold values from 0.25 to 1.75
- w_query: bfloat16 [4096, 4096], P('row', 'col')
- w_key: bfloat16 [4096, 4096], P('row', 'col')
- w_value: bfloat16 [4096, 4096], P('row', 'col'), may hold values from -0.09375 to 0.09375
- w_out: bfloat16 [4096, 4096], P('row', 'col'), may hold values from -0.75 to 0.75
Outputs:
- update: bfloat16 [8192, 4096], P('row', 'col')
The draws below stay inside these ranges and needn't reach their ends.
Inputs may be any that keep to these rules, and one draw needn't show every extreme that they name: `keep`: each row holds 64 different patch indices.
All inputs are finite; a program needn't handle non-finite values.
Results may differ from the reference program's by a relative error of at most 0.019.
Values may be sent and summed in bfloat16 or wider, within the bound.
No kernel may reach another device: no remote copies, remote signals or barrier semaphores. Data moves between devices by JAX's collectives and lax.ppermute only.
A program may use at most 128 MiB of HBM per device.

```python
import jax
import jax.numpy as jnp
from jax import lax

D = 4096
HEADS = 32
HEAD_DIM = 128
L = 256
KEEP = 64
POS = 1024
SEQS = 32
VIS = 2048


def draw_keep(key, part):
    key = jax.random.fold_in(key, 11)
    keys = jax.random.split(key, SEQS)
    return jax.vmap(lambda k: jax.random.permutation(k, L)[:KEEP])(keys).astype(jnp.int32)


def draw_w_query(key, part):
    key = jax.random.fold_in(key, 21)
    own = jax.random.normal(key, (D, D), jnp.float32)
    return (own * D ** (-0.5)).astype(jnp.bfloat16)


def draw_w_key(key, part):
    key = jax.random.fold_in(key, 31)
    own = jax.random.normal(key, (D, D), jnp.float32)
    return (own * D ** (-0.5)).astype(jnp.bfloat16)


def touch_ends(drawn, key, low, high):
    longest = drawn.shape.index(max(drawn.shape))
    spots = []
    for shift in (0, 1):
        where = [jax.random.randint(jax.random.fold_in(key, axis), (), 0, length) for axis, length in enumerate(drawn.shape)]
        where[longest] = (where[longest] + shift) % drawn.shape[longest]
        spots.append(tuple(where))
    return drawn.at[spots[0]].set(low).at[spots[1]].set(high)


def levels(stream_key, extent, shards, low, high):
    def one(position, blocks):
        draws = jax.random.uniform(jax.random.fold_in(jax.random.fold_in(stream_key, 6), position), (blocks,), jnp.float32, low / len(shards), high / len(shards))
        return jnp.repeat(jnp.exp(draws), extent[position] // blocks).reshape((-1,) + (1,) * (len(extent) - position - 1))

    level = one(*shards[0])
    for cut in shards[1:]:
        level = level * one(*cut)
    return level


def bell_draw(own_key, shape, width, reach, pieces=(), kind=jnp.bfloat16):
    level = levels(own_key, shape, pieces, -0.22, 0.18) if pieces else 1.0
    drawn = jax.random.normal(own_key, shape, jnp.float32) * width * level
    return jnp.minimum(jnp.maximum(drawn, -reach), reach).astype(kind)


def setup_inputs(seed: int = 0) -> dict:
    arg_keys = jax.random.split(jax.random.key(seed), 11)
    enc_out = bell_draw(arg_keys[0], (VIS, D), 1.0, 6.0, ((0, 32),))
    keep = draw_keep(jax.random.fold_in(arg_keys[10], 71), 0)
    pos_ids = touch_ends(jax.random.randint(arg_keys[2], (SEQS, L), 0, POS), jax.random.fold_in(arg_keys[2], 1), 0, POS - 1).astype(jnp.int32)
    mask_token = bell_draw(arg_keys[3], (D,), 1.0, 5.0, ((0, 4),))
    pos_table = bell_draw(arg_keys[4], (POS, D), 0.7, 4.0, ((1, 4),))
    gain = jnp.clip(1.0 + 0.15 * jax.random.normal(arg_keys[5], (D,), jnp.float32), 0.25, 1.75).astype(jnp.bfloat16)
    w_query = draw_w_query(jax.random.fold_in(arg_keys[10], 71), 0)
    w_key = draw_w_key(jax.random.fold_in(arg_keys[10], 71), 0)
    w_value = bell_draw(arg_keys[8], (D, D), D ** -0.5, 0.09375, ((0, 8), (1, 4)))
    w_out = bell_draw(arg_keys[9], (D, D), (D // 64) ** -0.5, 0.75, ((0, 8), (1, 4)))
    return dict(enc_out=enc_out, keep=keep, pos_ids=pos_ids, mask_token=mask_token, pos_table=pos_table, gain=gain, w_query=w_query, w_key=w_key, w_value=w_value, w_out=w_out)


EPS = 1e-05

def layer_norm(x, gain):
    xf = x.astype(jnp.float32)
    mean = lax.optimization_barrier(jnp.mean(xf, axis=-1, keepdims=True))
    var = lax.optimization_barrier(jnp.mean(xf * xf, axis=-1, keepdims=True)) - mean * mean
    return ((xf - mean) * lax.rsqrt(var + EPS) * gain.astype(jnp.float32)).astype(jnp.bfloat16)

def one_image(args):
    query, key, value = args
    scores = jnp.einsum('qhd,khd->hqk', query.astype(jnp.float32), key.astype(jnp.float32)) / jnp.sqrt(jnp.float32(HEAD_DIM))
    probs = jax.nn.softmax(scores, axis=-1).astype(jnp.bfloat16)
    attended = jnp.einsum('hqk,khd->qhd', probs.astype(jnp.float32), value.astype(jnp.float32))
    return attended.astype(jnp.bfloat16)

def reference(enc_out, keep, pos_ids, mask_token, pos_table, gain, w_query, w_key, w_value, w_out):
    images = keep.shape[0]
    base = jnp.broadcast_to(mask_token.astype(jnp.float32), (images, L, D))
    visible = enc_out.reshape(images, KEEP, D).astype(jnp.float32)
    which = jnp.arange(images, dtype=jnp.int32)[:, None]
    base = base.at[which, keep].set(visible)
    filled = (base + pos_table[pos_ids].astype(jnp.float32)).astype(jnp.bfloat16).reshape(images * L, D)
    normed = layer_norm(filled, gain)
    query = jnp.dot(normed, w_query, preferred_element_type=jnp.float32).astype(jnp.bfloat16)
    key = jnp.dot(normed, w_key, preferred_element_type=jnp.float32).astype(jnp.bfloat16)
    value = jnp.dot(normed, w_value, preferred_element_type=jnp.float32).astype(jnp.bfloat16)
    shape = (images, L, HEADS, HEAD_DIM)
    attended = lax.map(one_image, (query.reshape(shape), key.reshape(shape), value.reshape(shape)))
    attended = attended.reshape(images * L, D)
    return jnp.dot(attended, w_out, preferred_element_type=jnp.float32).astype(jnp.bfloat16)
```

```python
import functools

import jax
import jax.numpy as jnp
import numpy as np
from jax import lax
from jax.experimental import pallas as pl
from jax.experimental.pallas import tpu as pltpu
from jax.sharding import PartitionSpec as P

L = 256
HEAD_DIM = 128
EPS = 1e-05
BF = jnp.bfloat16
F32 = jnp.float32
MIB = 1 << 20


def after(x, *deps):
    return lax.optimization_barrier((x,) + deps)[0]


def row_offsets(rows):
    if rows == 8:
        even, odd = [0, 2, 4, 6, 1, 5, 3, 7], [0, 4, 2, 6, 1, 3, 5, 7]
        return [odd if r % 2 else even for r in range(rows)]
    return [list(range(rows)) for _ in range(rows)]


def row_slots(rows):
    slots = np.zeros((rows, rows), np.int32)
    for r, offsets in enumerate(row_offsets(rows)):
        for place, offset in enumerate(offsets):
            slots[r, r ^ offset] = place
    return slots


def swap(x, pairs):
    return lax.ppermute(x, "row", pairs)


def row_gather(x, rows):
    if rows == 8:
        first = [(r, r ^ (4 if r % 2 else 2)) for r in range(rows)]
        second = [(r, r ^ (2 if r % 2 else 4)) for r in range(rows)]
        sibling = [(r, r ^ 1) for r in range(rows)]
        a = swap(x, first)
        b = swap(x, second)
        c = swap(a, second)
        near = [x, a, b, c]
        return near + [swap(t, sibling) for t in near]
    blocks, bit = [x], 1
    while bit < rows:
        pairs = [(r, r ^ bit) for r in range(rows)]
        blocks = blocks + [swap(t, pairs) for t in blocks]
        bit *= 2
    return blocks


def shift(x, cols, step):
    return lax.ppermute(x, "col", [(c, (c + step) % cols) for c in range(cols)])


def col_gather(x, cols):
    blocks = [x] + [None] * (cols - 1)
    for k in range(1, cols // 2 + 1):
        blocks[k] = shift(blocks[k - 1], cols, 1)
    for k in range(cols - 1, cols // 2, -1):
        blocks[k] = shift(blocks[(k + 1) % cols], cols, -1)
    return blocks


def norm_kernel(
    rows, cols, slot_ref, col_ref, ids_ref, keep_ref, own_ref, *refs
):
    images = 4
    del images
    n_piece = (cols - 1) * rows
    pieces = refs[:n_piece]
    encs = refs[n_piece : n_piece + cols]
    gms = refs[n_piece + cols : n_piece + 2 * cols]
    out_ref, table, extra, held = refs[n_piece + 2 * cols :]
    image = pl.program_id(0)
    positions, width = own_ref.shape
    part = positions // rows
    vis = encs[0].shape[0]
    block = out_ref.shape[2]
    per = width // block

    @pl.when(image == 0)
    def _():
        me = col_ref[0]
        for b in range(rows):
            start = pl.multiple_of(slot_ref[b] * part, part)
            table[me, pl.ds(start, part), :] = own_ref[b * part : (b + 1) * part, :]
        for k in range(1, cols):
            source = col_ref[k]
            for p in range(rows):
                table[source, p * part : (p + 1) * part, :] = pieces[(k - 1) * rows + p][...]
        for k in range(cols):
            extra[col_ref[k]] = gms[k][...]
            for z in range(cols):
                low = positions + k * vis
                table[z, low : low + vis, :] = encs[k][:, z * width : (z + 1) * width]

    ids = ids_ref[...]
    wide = lax.broadcasted_iota(jnp.int32, (L, positions), 1)
    place = jnp.where(wide == ids, 1.0, 0.0).astype(BF)
    here = lax.broadcasted_iota(jnp.int32, (L, cols * vis), 0) + image * L
    seen = jnp.where(here == keep_ref[...], 1.0, 0.0)
    hidden = 1.0 - jnp.max(seen, axis=1, keepdims=True)
    pick = jnp.concatenate([place, seen.astype(BF)], axis=1)
    total = jnp.zeros((L, 1), F32)
    squares = jnp.zeros((L, 1), F32)
    for z in range(cols):
        x = jnp.dot(pick, table[z], preferred_element_type=F32)
        x = x + hidden * extra[z, 1:2, :].astype(F32)
        xb = x.astype(BF)
        held[z] = xb
        x = xb.astype(F32)
        total = total + jnp.sum(x, axis=1, keepdims=True)
        squares = squares + jnp.sum(x * x, axis=1, keepdims=True)
    mean = total / (cols * width)
    var = squares / (cols * width) - mean * mean
    scale = lax.rsqrt(var + EPS)
    for z in range(cols):
        x = held[z].astype(F32)
        y = ((x - mean) * scale * extra[z, 0:1, :].astype(F32)).astype(BF)
        for h in range(per):
            out_ref[slot_ref[z * per + h]] = y[:, h * block : (h + 1) * block]


def fill_and_norm(rows, cols, images, slot, order, ids, keep, own, pieces, encs, gms):
    positions, width = own.shape
    block = width * cols // rows
    vis = encs[0].shape[0]
    whole = lambda a: pl.BlockSpec(a.shape, lambda i, *_: (0,) * a.ndim)
    operands = [ids, keep, own] + pieces + encs + gms
    specs = [pl.BlockSpec((L, 1), lambda i, *_: (i, 0))] + [whole(a) for a in operands[1:]]
    return pl.pallas_call(
        functools.partial(norm_kernel, rows, cols),
        out_shape=jax.ShapeDtypeStruct((rows, images * L, block), BF),
        grid_spec=pltpu.PrefetchScalarGridSpec(
            num_scalar_prefetch=2,
            grid=(images,),
            in_specs=specs,
            out_specs=pl.BlockSpec((rows, L, block), lambda i, *_: (0, i, 0)),
            scratch_shapes=[
                pltpu.VMEM((cols, positions + cols * vis, width), BF),
                pltpu.VMEM((cols,) + gms[0].shape, BF),
                pltpu.VMEM((cols, L, width), BF),
            ],
        ),
        compiler_params=pltpu.CompilerParams(vmem_limit_bytes=60 * MIB),
        cost_estimate=pl.CostEstimate(
            flops=2 * images * L * (positions + cols * vis) * width * cols,
            bytes_accessed=24 * MIB,
            transcendentals=0,
        ),
        name="fill_norm",
    )(slot, order, *operands)


def heads_kernel(rows, heads, x_ref, *refs):
    weights, out_ref = refs[:rows], refs[rows]
    acc = None
    for p in range(rows):
        term = jnp.dot(x_ref[p], weights[p][...], preferred_element_type=F32)
        acc = term if acc is None else acc + term
    acc = acc.astype(BF)
    hw = heads * HEAD_DIM
    scale = HEAD_DIM**-0.5
    for h in range(heads):
        cut = lambda j: acc[:, j * hw + h * HEAD_DIM : j * hw + (h + 1) * HEAD_DIM]
        s = lax.dot_general(
            cut(0), cut(1), (((1,), (1,)), ((), ())), preferred_element_type=F32
        ) * scale
        e = jnp.exp(s - jnp.max(s, axis=1, keepdims=True))
        p = (e / jnp.sum(e, axis=1, keepdims=True)).astype(BF)
        o = jnp.dot(p, cut(2), preferred_element_type=F32)
        out_ref[:, h * HEAD_DIM : (h + 1) * HEAD_DIM] = o.astype(BF)


def some_heads(normed, weights, heads):
    rows, tokens, block = normed.shape
    hw = heads * HEAD_DIM
    return pl.pallas_call(
        functools.partial(heads_kernel, rows, heads),
        out_shape=jax.ShapeDtypeStruct((tokens, hw), BF),
        grid=(tokens // L,),
        in_specs=[pl.BlockSpec((rows, L, block), lambda i: (0, i, 0))]
        + [pl.BlockSpec(w.shape, lambda i: (0, 0)) for w in weights],
        out_specs=pl.BlockSpec((L, hw), lambda i: (i, 0)),
        compiler_params=pltpu.CompilerParams(vmem_limit_bytes=48 * MIB),
        cost_estimate=pl.CostEstimate(
            flops=2 * tokens * rows * block * 3 * hw + 4 * tokens * L * hw,
            bytes_accessed=2 * tokens * rows * block + 6 * rows * block * hw + 2 * tokens * hw,
            transcendentals=tokens * L * heads,
        ),
        name=f"heads_{heads}",
    )(normed, *weights)


def out_kernel(n, has_acc, at_ref, *refs):
    xs, ws = refs[:n], refs[n : 2 * n]
    out_ref = refs[-1]
    acc = refs[2 * n][...] if has_acc else None
    for x_ref, w_ref in zip(xs, ws):
        term = jnp.dot(x_ref[...], w_ref[0], preferred_element_type=F32)
        acc = term if acc is None else acc + term
    out_ref[...] = acc.astype(out_ref.dtype)


def project(at, xs, stacked, inner, acc, last):
    n = len(xs)
    tokens, depth = xs[0].shape
    width = stacked.shape[2]
    row = lambda i, *_: (i, 0)
    specs = [pl.BlockSpec((L, depth), row)] * n
    for k in range(n):
        specs.append(
            pl.BlockSpec((1, depth, width), lambda i, at, k=k: (at[k], inner // depth, 0))
        )
    operands = list(xs) + [stacked] * n
    alias = {}
    if acc is not None:
        specs.append(pl.BlockSpec((L, width), row))
        operands.append(acc)
        if not last:
            alias = {1 + 2 * n: 0}
    return pl.pallas_call(
        functools.partial(out_kernel, n, acc is not None),
        out_shape=jax.ShapeDtypeStruct((tokens, width), BF if last else F32),
        grid_spec=pltpu.PrefetchScalarGridSpec(
            num_scalar_prefetch=1,
            grid=(tokens // L,),
            in_specs=specs,
            out_specs=pl.BlockSpec((L, width), row),
        ),
        input_output_aliases=alias,
        compiler_params=pltpu.CompilerParams(vmem_limit_bytes=32 * MIB),
        cost_estimate=pl.CostEstimate(
            flops=2 * tokens * depth * n * width,
            bytes_accessed=2 * n * depth * (tokens + width) + 8 * tokens * width,
            transcendentals=0,
        ),
        name="out_proj",
    )(at, *operands)


def head_chunks(heads):
    chunks, low = [], 0
    for size in [1, 1] + [2] * heads:
        if low >= heads:
            break
        size = min(size, heads - low)
        chunks.append((low, size))
        low += size
    return chunks


def on_device(
    rows, cols, enc_out, keep, pos_ids, mask_token, pos_table, gain, w_query, w_key, w_value, w_out
):
    images = keep.shape[0]
    positions, width = pos_table.shape
    r, c = lax.axis_index("row"), lax.axis_index("col")
    slot = jnp.asarray(row_slots(rows))[r]
    order = (c - jnp.arange(cols, dtype=jnp.int32)) % cols
    chunks = head_chunks(width // HEAD_DIM)

    def packed(low, size):
        cut = slice(low * HEAD_DIM, (low + size) * HEAD_DIM)
        return jnp.concatenate([w_query[:, cut], w_key[:, cut], w_value[:, cut]], axis=1)

    part = positions // rows
    share = lax.dynamic_slice_in_dim(pos_table, r * part, part, axis=0)
    pad = jnp.zeros((14, width), BF)
    share = jnp.concatenate([share, gain[None], mask_token[None], pad], axis=0)
    shares = col_gather(share, cols)
    gms = [s[part : part + 16] for s in shares]

    enc = after(enc_out, shares[1], shares[cols - 1])
    encs = col_gather(enc, cols)

    gathered = []
    gathered.append(row_gather(packed(*chunks[0]), rows))
    pieces = []
    for k in range(1, cols):
        pieces.append(row_gather(shares[k][:part], rows))
    prev = [gathered[0][3], pieces[-1][3]]
    for low, size in chunks[1:]:
        w = after(packed(low, size), prev[-2])
        gathered.append(row_gather(w, rows))
        prev.append(gathered[-1][3])
    w_outs = row_gather(after(w_out, prev[-2]), rows)
    stacked = jnp.stack(w_outs)

    ids = (slot[pos_ids // part] * part + pos_ids % part).reshape(images * L, 1)
    numbers = keep + L * jnp.arange(images, dtype=jnp.int32)[:, None]
    numbers = numbers.reshape(cols, -1)[order].reshape(1, -1)

    normed = fill_and_norm(
        rows, cols, images, slot, order, ids, numbers, pos_table,
        [p for piece in pieces for p in piece], encs, gms,
    )

    acc = None
    block = w_out.shape[0]
    for (low, size), weights in zip(chunks, gathered):
        attended = some_heads(normed, weights, size)
        xs = col_gather(attended, cols)
        first = low * HEAD_DIM
        at = slot[(order * width + first) // block]
        last = (low, size) == chunks[-1]
        acc = project(at, xs, stacked, first % block, acc, last)
    return acc


def solution(mesh):
    rows, cols = mesh.shape["row"], mesh.shape["col"]
    in_specs = (
        P(("row", "col"), None),
        P("row", None),
        P("row", None),
        P("col"),
        P(None, "col"),
        P("col"),
        P("row", "col"),
        P("row", "col"),
        P("row", "col"),
        P("row", "col"),
    )
    return jax.shard_map(
        functools.partial(on_device, rows, cols),
        mesh=mesh,
        in_specs=in_specs,
        out_specs=P("row", "col"),
        check_vma=False,
    )
```

```python
import functools

import jax
import jax.numpy as jnp
import numpy as np
from jax import lax
from jax.experimental import pallas as pl
from jax.experimental.pallas import tpu as pltpu
from jax.sharding import PartitionSpec as P

L = 256
HEAD_DIM = 128
EPS = 1e-05
BF = jnp.bfloat16
F32 = jnp.float32
MIB = 1 << 20
VMEM = 60 * MIB
LIGHT = pl.CostEstimate(flops=1, bytes_accessed=1, transcendentals=0)


def after(x, *deps):
    return lax.optimization_barrier((x,) + deps)[0]


def row_offsets(rows):
    if rows == 8:
        even, odd = [0, 2, 4, 6, 1, 5, 3, 7], [0, 4, 2, 6, 1, 3, 5, 7]
        return [odd if r % 2 else even for r in range(rows)]
    offsets, bit = [0], rows // 2
    while bit:
        offsets = offsets + [t ^ bit for t in offsets]
        bit //= 2
    return [offsets] * rows


def row_slots(rows):
    slots = np.zeros((rows, rows), np.int32)
    for r, offsets in enumerate(row_offsets(rows)):
        for place, offset in enumerate(offsets):
            slots[r, r ^ offset] = place
    return slots


def row_sources(rows):
    return np.array([[r ^ t for t in row] for r, row in enumerate(row_offsets(rows))], np.int32)


def swap(x, pairs):
    return lax.ppermute(x, "row", pairs)


class Rows:
    def __init__(self, x, rows):
        self.rows, self.x = rows, x
        self.parts = {0: x}
        self.first = [(r, r ^ (4 if r % 2 else 2)) for r in range(rows)]
        self.second = [(r, r ^ (2 if r % 2 else 4)) for r in range(rows)]
        self.sibling = [(r, r ^ 1) for r in range(rows)]

    def fetch(self, *places):
        for p in places:
            pairs = {1: self.first, 2: self.second, 3: self.second}.get(p, self.sibling)
            origin = {1: 0, 2: 0, 3: 1}.get(p, p - 4)
            self.parts[p] = swap(self.parts[origin], pairs)

    def start(self):
        if self.rows == 8:
            self.fetch(1, 2, 4)
            return
        blocks, bit = [self.x], self.rows // 2
        while bit:
            pairs = [(r, r ^ bit) for r in range(self.rows)]
            blocks = blocks + [swap(t, pairs) for t in blocks]
            bit //= 2
        self.parts = dict(enumerate(blocks))

    def forward(self):
        if self.rows == 8:
            self.fetch(3, 5, 6)

    def finish(self):
        if self.rows == 8:
            self.fetch(7)

    def blocks(self, places):
        return [self.parts[p] for p in places]


def early_places(rows):
    return [0, 1, 2, 4] if rows == 8 else list(range(rows // 2))


def shift(x, cols, step):
    return lax.ppermute(x, "col", [(c, (c + step) % cols) for c in range(cols)])


def near_cols(x, cols):
    blocks = [x] + [None] * (cols - 1)
    blocks[1] = shift(x, cols, 1)
    if cols > 2:
        blocks[cols - 1] = shift(x, cols, -1)
    return blocks


def far_cols(blocks, cols):
    blocks = list(blocks)
    for k in range(2, cols // 2 + 1):
        if blocks[k] is None:
            blocks[k] = shift(blocks[k - 1], cols, 1)
    for k in range(cols - 2, cols // 2, -1):
        blocks[k] = shift(blocks[k + 1], cols, -1)
    return blocks


def col_gather(x, cols):
    return far_cols(near_cols(x, cols), cols)


def place_kernel(parts, ids_ref, *refs):
    tables, out_ref, held = refs[: sum(parts)], refs[-2], refs[-1]
    width = out_ref.shape[1]

    @pl.when(pl.program_id(0) == 0)
    def _():
        column, at = 0, 0
        for count in parts:
            low = 0
            for block in tables[at : at + count]:
                held[low : low + block.shape[0], column : column + block.shape[1]] = block[...]
                low += block.shape[0]
            at += count
            column += block.shape[1]

    wide = lax.broadcasted_iota(jnp.int32, (L, held.shape[0]), 1)
    pick = jnp.where(wide == ids_ref[...], 1.0, 0.0).astype(BF)
    step = min(width, 1024)
    for low in range(0, width, step):
        out_ref[:, low : low + step] = jnp.dot(
            pick, held[:, low : low + step], preferred_element_type=F32
        ).astype(BF)


def place(ids, *tables):
    tokens = ids.shape[0]
    positions = sum(t.shape[0] for t in tables[0])
    width = sum(t[0].shape[1] for t in tables)
    operands = [t for table in tables for t in table]
    return pl.pallas_call(
        functools.partial(place_kernel, [len(t) for t in tables]),
        out_shape=jax.ShapeDtypeStruct((tokens, width), BF),
        grid=(tokens // L,),
        in_specs=[pl.BlockSpec((L, 1), lambda i: (i, 0))]
        + [pl.BlockSpec(t.shape, lambda i: (0, 0)) for t in operands],
        out_specs=pl.BlockSpec((L, width), lambda i: (i, 0)),
        scratch_shapes=[pltpu.VMEM((positions, width), BF)],
        compiler_params=pltpu.CompilerParams(vmem_limit_bytes=VMEM),
        cost_estimate=LIGHT,
        name="place",
    )(ids, *operands)


def norm_kernel(cols, part, n_late, col_ref, keep_ref, ids_ref, own_ref, near_ref, *refs):
    late, refs = refs[:n_late], refs[n_late:]
    encs, shares = refs[:cols], refs[cols : 2 * cols]
    out_ref, extra, table, held = refs[2 * cols :]
    image = pl.program_id(0)
    width = held.shape[2]
    vis = encs[0].shape[0]
    seen_all = cols * vis
    base = seen_all + 128

    @pl.when(image == 0)
    def _():
        for k in range(cols):
            both = shares[k][part : part + 16, :]
            extra[k] = both
            at = col_ref[k]
            table[at, seen_all : seen_all + 16, :] = both
            table[at, seen_all + 16 : base, :] = jnp.zeros((112, width), BF)
            for z in range(cols):
                table[z, k * vis : (k + 1) * vis, :] = encs[k][:, z * width : (z + 1) * width]
            if k:
                for p in range(n_late):
                    low = base + p * part
                    table[at, low : low + part, :] = late[p][:, (k - 1) * width : k * width]

    here = lax.broadcasted_iota(jnp.int32, (L, seen_all), 0) + image * L
    seen = jnp.where(here == keep_ref[...], 1.0, 0.0)
    hidden = 1.0 - jnp.max(seen, axis=1, keepdims=True)
    lane = lax.broadcasted_iota(jnp.int32, (L, 128), 1)
    wide = lax.broadcasted_iota(jnp.int32, (L, n_late * part), 1)
    rest = jnp.where(wide == ids_ref[...], 1.0, 0.0)
    pick = jnp.concatenate([seen, jnp.where(lane == 1, hidden, 0.0), rest], axis=1).astype(BF)
    ones = jnp.ones((width, 128), BF)
    total = jnp.zeros((L, 128), F32)
    squares = jnp.zeros((L, 1), F32)
    for k in range(cols):
        at = col_ref[k]
        if k == 0:
            x = jnp.dot(pick[:, :base], table[at, :base, :], preferred_element_type=F32)
            x = x + own_ref[...].astype(F32)
        else:
            x = jnp.dot(pick, table[at], preferred_element_type=F32)
            x = x + near_ref[:, (k - 1) * width : k * width].astype(F32)
        xb = x.astype(BF)
        held[k] = xb
        total = total + jnp.dot(xb, ones, preferred_element_type=F32)
        x = xb.astype(F32)
        squares = squares + jnp.sum(x * x, axis=1, keepdims=True)
    mean = total[:, :1] / (cols * width)
    var = squares / (cols * width) - mean * mean
    scale = lax.rsqrt(var + EPS)
    for k in range(cols):
        x = held[k].astype(F32)
        low = pl.multiple_of(col_ref[k] * width, width)
        out_ref[:, pl.ds(low, width)] = (
            (x - mean) * scale * extra[k, 0:1, :].astype(F32)
        ).astype(BF)


def fill_and_norm(part, order, keep, ids, own, near, late, encs, shares):
    tokens, width = own.shape
    cols = len(encs)
    vis = encs[0].shape[0]
    whole = lambda a: pl.BlockSpec(a.shape, lambda i, *_: (0, 0))
    row = lambda i, *_: (i, 0)
    return pl.pallas_call(
        functools.partial(norm_kernel, cols, part, len(late)),
        out_shape=jax.ShapeDtypeStruct((tokens, cols * width), BF),
        grid_spec=pltpu.PrefetchScalarGridSpec(
            num_scalar_prefetch=1,
            grid=(tokens // L,),
            in_specs=[whole(keep)]
            + [pl.BlockSpec((L, p.shape[1]), row) for p in (ids, own, near)]
            + [whole(a) for a in late + encs + shares],
            out_specs=pl.BlockSpec((L, cols * width), row),
            scratch_shapes=[
                pltpu.VMEM((cols, 16, width), BF),
                pltpu.VMEM((cols, cols * vis + 128 + len(late) * part, width), BF),
                pltpu.VMEM((cols, L, width), BF),
            ],
        ),
        compiler_params=pltpu.CompilerParams(vmem_limit_bytes=VMEM),
        cost_estimate=LIGHT,
        name="fill_norm",
    )(order, keep, ids, own, near, *late, *encs, *shares)


def attend(projected, heads, out_ref):
    hw = heads * HEAD_DIM
    scale = HEAD_DIM**-0.5
    for h in range(heads):
        cut = lambda j: projected[:, j * hw + h * HEAD_DIM : j * hw + (h + 1) * HEAD_DIM]
        s = lax.dot_general(
            cut(0), cut(1), (((1,), (1,)), ((), ())), preferred_element_type=F32
        ) * scale
        e = jnp.exp(s - jnp.max(s, axis=1, keepdims=True))
        p = (e / jnp.sum(e, axis=1, keepdims=True)).astype(BF)
        o = jnp.dot(p, cut(2), preferred_element_type=F32)
        out_ref[:, h * HEAD_DIM : (h + 1) * HEAD_DIM] = o.astype(BF)


def heads_kernel(heads, source_ref, x_ref, *refs):
    weights, out_ref = refs[:-1], refs[-1]
    if len(weights) == 1:
        acc = jnp.dot(x_ref[...], weights[0][...], preferred_element_type=F32)
    else:
        acc = None
        for p, w_ref in enumerate(weights):
            block = w_ref.shape[0]
            low = pl.multiple_of(source_ref[p] * block, block)
            term = jnp.dot(x_ref[:, pl.ds(low, block)], w_ref[...], preferred_element_type=F32)
            acc = term if acc is None else acc + term
    attend(acc.astype(BF), heads, out_ref)


def some_heads(source, normed, weights, heads):
    tokens, depth = normed.shape
    hw = heads * HEAD_DIM
    return pl.pallas_call(
        functools.partial(heads_kernel, heads),
        out_shape=jax.ShapeDtypeStruct((tokens, hw), BF),
        grid_spec=pltpu.PrefetchScalarGridSpec(
            num_scalar_prefetch=1,
            grid=(tokens // L,),
            in_specs=[pl.BlockSpec((L, depth), lambda i, *_: (i, 0))]
            + [pl.BlockSpec(w.shape, lambda i, *_: (0, 0)) for w in weights],
            out_specs=pl.BlockSpec((L, hw), lambda i, *_: (i, 0)),
        ),
        compiler_params=pltpu.CompilerParams(vmem_limit_bytes=VMEM),
        cost_estimate=LIGHT,
        name=f"heads_{heads}",
    )(source, normed, *weights)


def out_kernel(n, has_acc, at_ref, *refs):
    xs, ws = refs[:n], refs[n : 2 * n]
    out_ref = refs[-1]
    acc = refs[2 * n][...] if has_acc else None
    for x_ref, w_ref in zip(xs, ws):
        term = jnp.dot(x_ref[...], w_ref[...], preferred_element_type=F32)
        acc = term if acc is None else acc + term
    out_ref[...] = acc.astype(out_ref.dtype)


def project(order, groups, weight, acc, last):
    tokens = next(iter(groups[0][1].values())).shape[0]
    width = weight.shape[1]
    row = lambda i, *_: (i, 0)
    xs, x_specs, w_specs = [], [], []
    for first, parts in groups:
        depth = parts[min(parts)].shape[1]
        for k, x in sorted(parts.items()):
            xs.append(x)
            x_specs.append(pl.BlockSpec((L, depth), row))
            w_specs.append(
                pl.BlockSpec(
                    (depth, width),
                    lambda i, at, k=k, first=first, depth=depth: (
                        at[k] * (width // depth) + first // depth, 0
                    ),
                )
            )
    n = len(xs)
    operands = xs + [weight] * n
    specs = x_specs + w_specs
    alias = {}
    if acc is not None:
        specs.append(pl.BlockSpec((L, width), row))
        operands.append(acc)
        if not last:
            alias = {1 + 2 * n: 0}
    depths = sum(x.shape[1] for x in xs)
    return pl.pallas_call(
        functools.partial(out_kernel, n, acc is not None),
        out_shape=jax.ShapeDtypeStruct((tokens, width), BF if last else F32),
        grid_spec=pltpu.PrefetchScalarGridSpec(
            num_scalar_prefetch=1,
            grid=(tokens // L,),
            in_specs=specs,
            out_specs=pl.BlockSpec((L, width), row),
        ),
        input_output_aliases=alias,
        compiler_params=pltpu.CompilerParams(vmem_limit_bytes=VMEM),
        cost_estimate=LIGHT,
        name="out_proj",
    )(order, *operands)


def head_chunks(heads):
    return [(low, 2) for low in range(0, heads, 2)]


def gate(*trees):
    return lax.optimization_barrier(trees)


def on_device(
    rows, cols, enc_out, keep, pos_ids, mask_token, pos_table, gain, w_query, w_key, w_value, w_out
):
    images = keep.shape[0]
    positions, width = pos_table.shape
    r, c = lax.axis_index("row"), lax.axis_index("col")
    slot = jnp.asarray(row_slots(rows))[r]
    order = (c - jnp.arange(cols, dtype=jnp.int32)) % cols
    chunks = head_chunks(width // HEAD_DIM)
    n = len(chunks)

    def packed(k):
        low, size = chunks[k]
        cut = slice(low * HEAD_DIM, (low + size) * HEAD_DIM)
        return jnp.concatenate([w_query[:, cut], w_key[:, cut], w_value[:, cut]], axis=1)

    part = positions // rows
    owner, inner = pos_ids // part, pos_ids % part
    early = early_places(rows)
    later = [p for p in range(rows) if p not in early]

    def ids_of(places):
        rank = np.full((rows,), -rows, np.int32)
        rank[places] = np.arange(len(places))
        rank = jnp.asarray(rank[row_slots(rows)])[r]
        ids = inner
        for b in range(rows):
            ids = ids + jnp.where(owner == b, rank[b] * part, 0)
        return ids.reshape(images * L, 1)

    small = (
        pos_ids.reshape(images * L, 1),
        ids_of(early),
        ids_of(later),
        (keep + L * jnp.arange(images, dtype=jnp.int32)[:, None]).reshape(cols, -1)[order].reshape(1, -1),
        jnp.asarray(row_sources(rows))[r],
        order,
    )

    share = lax.dynamic_slice_in_dim(pos_table, r * part, part, axis=0)
    pad = jnp.zeros((14, width), BF)
    share = jnp.concatenate([share, gain[None], mask_token[None], pad], axis=0)
    others = range(1, cols)

    gather = lambda w: lax.all_gather(w, "row", axis=0, tiled=True)
    split = rows == 8 and n >= 4
    weights = [[gather(packed(0))]]
    shares = [share] + [shift(share, cols, k) for k in others]
    placed_own = place(small[0], [pos_table])
    packs = [packed(k) for k in range(1, n)]
    shares, placed_own, enc, packs, w_out, small = gate(
        shares, placed_own, enc_out, packs, w_out, small
    )
    _, early_ids, later_ids, numbers, source, order = small

    weights += [[gather(p)] for p in (packs[:-1] if split else packs)]
    w_full = gather(w_out)
    late = Rows(packs[-1], rows)

    table = Rows(jnp.concatenate([shares[k][:part] for k in others], axis=1), rows)
    table.start()
    encs = near_cols(enc, cols)
    table.parts, encs = gate(table.parts, encs)

    encs = far_cols(encs, cols)
    table.forward()
    placed = place(early_ids, table.blocks(early))
    table.parts, encs, placed = gate(table.parts, encs, placed)

    table.finish()
    if split:
        late.fetch(1, 2)
    normed = fill_and_norm(
        part, order, numbers, later_ids, placed_own, placed, table.blocks(later), encs, shares
    )
    attended = some_heads(source, normed, weights[0], chunks[0][1])
    attended, normed, late.parts = gate(attended, normed, late.parts)

    sent, half = [], None
    for k in range(1, n):
        whole = far_cols(half, cols) if half else None
        half = near_cols(attended, cols)
        if split and k == 1:
            late.fetch(3, 5)
        if split and k == 2:
            late.fetch(4, 6, 7)
        if split and k == n - 1:
            weights.append(late.blocks(range(rows)))
        attended = some_heads(source, normed, weights[k], chunks[k][1])
        attended, normed, half, whole, late.parts = gate(attended, normed, half, whole, late.parts)
        if whole:
            sent.append(whole)
    group = lambda k: (chunks[k][0] * HEAD_DIM, dict(enumerate(sent[k])))
    whole = far_cols(half, cols)
    half = near_cols(attended, cols)
    acc = None
    if n > 2:
        acc = project(order, [group(k) for k in range(n - 2)], w_full, None, False)
    half, whole, acc = gate(half, whole, acc)
    sent.append(whole)
    first = chunks[n - 1][0] * HEAD_DIM
    here = {k: x for k, x in enumerate(half) if x is not None}
    acc = project(order, [group(n - 2), (first, here)], w_full, acc, False)
    far = {k: x for k, x in enumerate(far_cols(half, cols)) if k not in here}
    return project(order, [(first, far)], w_full, acc, True)


def solution(mesh):
    rows, cols = mesh.shape["row"], mesh.shape["col"]
    in_specs = (
        P(("row", "col"), None),
        P("row", None),
        P("row", None),
        P("col"),
        P(None, "col"),
        P("col"),
        P("row", "col"),
        P("row", "col"),
        P("row", "col"),
        P("row", "col"),
    )
    return jax.shard_map(
        functools.partial(on_device, rows, cols),
        mesh=mesh,
        in_specs=in_specs,
        out_specs=P("row", "col"),
        check_vma=False,
    )
```

```python
import functools

import jax
import jax.numpy as jnp
import numpy as np
from jax import lax
from jax.experimental import pallas as pl
from jax.experimental.pallas import tpu as pltpu
from jax.sharding import PartitionSpec as P

L = 256
HEAD_DIM = 128
EPS = 1e-05
BF = jnp.bfloat16
F32 = jnp.float32
MIB = 1 << 20
VMEM = 60 * MIB
LIGHT = pl.CostEstimate(flops=1, bytes_accessed=1, transcendentals=0)


def after(x, *deps):
    return lax.optimization_barrier((x,) + deps)[0]


def row_offsets(rows):
    if rows == 8:
        even, odd = [0, 2, 4, 6, 1, 5, 3, 7], [0, 4, 2, 6, 1, 3, 5, 7]
        return [odd if r % 2 else even for r in range(rows)]
    offsets, bit = [0], rows // 2
    while bit:
        offsets = offsets + [t ^ bit for t in offsets]
        bit //= 2
    return [offsets] * rows


def swap(x, pairs):
    return lax.ppermute(x, "row", pairs)


class Rows:
    def __init__(self, x, rows):
        self.rows, self.x = rows, x
        self.parts = {0: x}
        self.first = [(r, r ^ (4 if r % 2 else 2)) for r in range(rows)]
        self.second = [(r, r ^ (2 if r % 2 else 4)) for r in range(rows)]
        self.sibling = [(r, r ^ 1) for r in range(rows)]

    def fetch(self, *places):
        for p in places:
            pairs = {1: self.first, 2: self.second, 3: self.second}.get(p, self.sibling)
            origin = {1: 0, 2: 0, 3: 1}.get(p, p - 4)
            self.parts[p] = swap(self.parts[origin], pairs)

    def start(self):
        if self.rows == 8:
            self.fetch(1, 2, 4)
            return
        blocks, bit = [self.x], self.rows // 2
        while bit:
            pairs = [(r, r ^ bit) for r in range(self.rows)]
            blocks = blocks + [swap(t, pairs) for t in blocks]
            bit //= 2
        self.parts = dict(enumerate(blocks))

    def forward(self):
        if self.rows == 8:
            self.fetch(3, 5, 6)

    def finish(self):
        if self.rows == 8:
            self.fetch(7)

    def blocks(self, places):
        return [self.parts[p] for p in places]


def early_places(rows):
    return [0, 1, 2, 4] if rows == 8 else list(range(rows // 2))


def shift(x, cols, step):
    return lax.ppermute(x, "col", [(c, (c + step) % cols) for c in range(cols)])


def near_cols(x, cols):
    blocks = [x] + [None] * (cols - 1)
    blocks[1] = shift(x, cols, 1)
    if cols > 2:
        blocks[cols - 1] = shift(x, cols, -1)
    return blocks


def far_cols(blocks, cols):
    blocks = list(blocks)
    for k in range(2, cols // 2 + 1):
        if blocks[k] is None:
            blocks[k] = shift(blocks[k - 1], cols, 1)
    for k in range(cols - 2, cols // 2, -1):
        blocks[k] = shift(blocks[k + 1], cols, -1)
    return blocks


def col_gather(x, cols):
    return far_cols(near_cols(x, cols), cols)


def pack_kernel(count, *refs):
    for k in range(len(refs) // (count + 1)):
        out_ref = refs[len(refs) * count // (count + 1) + k]
        width = out_ref.shape[1] // count
        for j in range(count):
            out_ref[:, j * width : (j + 1) * width] = refs[k * count + j][...]


def pack(weights, chunks):
    depth = weights[0].shape[0]
    in_specs, out_specs, shapes = [], [], []
    for low, size in chunks:
        width = size * HEAD_DIM
        spec = pl.BlockSpec((depth, width), lambda i, at=low // size: (0, at))
        in_specs += [spec] * len(weights)
        wide = (depth, width * len(weights))
        out_specs.append(pl.BlockSpec(wide, lambda i: (0, 0)))
        shapes.append(jax.ShapeDtypeStruct(wide, BF))
    return pl.pallas_call(
        functools.partial(pack_kernel, len(weights)),
        out_shape=shapes,
        grid=(1,),
        in_specs=in_specs,
        out_specs=out_specs,
        compiler_params=pltpu.CompilerParams(vmem_limit_bytes=VMEM),
        cost_estimate=LIGHT,
        name="pack",
    )(*(list(weights) * len(chunks)))


def attend(projected, heads, out_ref):
    hw = heads * HEAD_DIM
    scale = HEAD_DIM**-0.5
    cut = lambda j, h: projected[:, j * hw + h * HEAD_DIM : j * hw + (h + 1) * HEAD_DIM]
    scores = [
        lax.dot_general(
            cut(0, h), cut(1, h), (((1,), (1,)), ((), ())), preferred_element_type=F32
        ) * scale
        for h in range(heads)
    ]
    raised = [jnp.exp(s - jnp.max(s, axis=1, keepdims=True)) for s in scores]
    probs = [(e * (1.0 / jnp.sum(e, axis=1, keepdims=True))).astype(BF) for e in raised]
    out = [jnp.dot(p, cut(2, h), preferred_element_type=F32) for h, p in enumerate(probs)]
    out_ref[...] = jnp.concatenate(out, axis=1).astype(BF)


def place_kernel(parts, column_of_ids, ids_ref, *refs):
    tables, out_ref, held = refs[: sum(parts)], refs[-2], refs[-1]
    width = out_ref.shape[1]

    @pl.when(pl.program_id(0) == 0)
    def _():
        column, at = 0, 0
        for count in parts:
            low = 0
            for block in tables[at : at + count]:
                held[low : low + block.shape[0], column : column + block.shape[1]] = block[...]
                low += block.shape[0]
            at += count
            column += block.shape[1]

    wide = lax.broadcasted_iota(jnp.int32, (L, held.shape[0]), 1)
    ids = ids_ref[:, column_of_ids : column_of_ids + 1]
    pick = jnp.where(wide == ids, 1.0, 0.0).astype(BF)
    step = min(width, 1024)
    for low in range(0, width, step):
        out_ref[:, low : low + step] = jnp.dot(
            pick, held[:, low : low + step], preferred_element_type=F32
        ).astype(BF)


def place(ids, which, *tables):
    tokens = ids.shape[0]
    positions = sum(t.shape[0] for t in tables[0])
    width = sum(t[0].shape[1] for t in tables)
    operands = [t for table in tables for t in table]
    return pl.pallas_call(
        functools.partial(place_kernel, [len(t) for t in tables], which),
        out_shape=jax.ShapeDtypeStruct((tokens, width), BF),
        grid=(tokens // L,),
        in_specs=[pl.BlockSpec((L, ids.shape[1]), lambda i: (i, 0))]
        + [pl.BlockSpec(t.shape, lambda i: (0, 0)) for t in operands],
        out_specs=pl.BlockSpec((L, width), lambda i: (i, 0)),
        scratch_shapes=[pltpu.VMEM((positions, width), BF)],
        compiler_params=pltpu.CompilerParams(vmem_limit_bytes=VMEM),
        cost_estimate=LIGHT,
        name="place",
    )(ids, *operands)


def norm_kernel(cols, part, n_late, col_ref, keep_ref, ids_ref, own_ref, near_ref, *refs):
    late, weights, refs = refs[:n_late], refs[n_late], refs[n_late + 1 :]
    encs, shares = refs[:cols], refs[cols : 2 * cols]
    out_ref, attended_ref, extra, table, held = refs[2 * cols :]
    image = pl.program_id(0)
    width = held.shape[2]
    vis = encs[0].shape[0]
    seen_all = cols * vis
    base = seen_all + 128

    @pl.when(image == 0)
    def _():
        for k in range(cols):
            both = shares[k][part : part + 16, :]
            extra[k] = both
            at = col_ref[k]
            table[at, seen_all : seen_all + 16, :] = both
            table[at, seen_all + 16 : base, :] = jnp.zeros((112, width), BF)
            for z in range(cols):
                table[z, k * vis : (k + 1) * vis, :] = encs[k][:, z * width : (z + 1) * width]
            if k:
                for p in range(n_late):
                    low = base + p * part
                    table[at, low : low + part, :] = late[p][:, (k - 1) * width : k * width]

    here = lax.broadcasted_iota(jnp.int32, (L, seen_all), 0) + image * L
    seen = jnp.where(here == keep_ref[...], 1.0, 0.0)
    hidden = 1.0 - jnp.max(seen, axis=1, keepdims=True)
    lane = lax.broadcasted_iota(jnp.int32, (L, 128), 1)
    wide = lax.broadcasted_iota(jnp.int32, (L, n_late * part), 1)
    rest = jnp.where(wide == ids_ref[:, 2:3], 1.0, 0.0)
    pick = jnp.concatenate([seen, jnp.where(lane == 1, hidden, 0.0), rest], axis=1).astype(BF)
    def filled(k):
        at = col_ref[k]
        if k == 0:
            return jnp.dot(pick[:, :base], table[at, :base, :], preferred_element_type=F32)
        return jnp.dot(pick, table[at], preferred_element_type=F32)

    squares = jnp.zeros((L, 1), F32)
    total = jnp.zeros((L, 1), F32)
    products = [filled(0)]
    for k in range(cols):
        if k + 1 < cols:
            products.append(filled(k + 1))
        placed = own_ref[...] if k == 0 else near_ref[:, (k - 1) * width : k * width]
        xb = (products[k] + placed.astype(F32)).astype(BF)
        held[k] = xb
        x = xb.astype(F32)
        total = total + jnp.sum(x, axis=1, keepdims=True)
        squares = squares + jnp.sum(x * x, axis=1, keepdims=True)
    mean = total / (cols * width)
    var = squares / (cols * width) - mean * mean
    scale = lax.rsqrt(var + EPS)
    for k in range(cols):
        x = held[k].astype(F32)
        low = pl.multiple_of(col_ref[k] * width, width)
        out_ref[:, pl.ds(low, width)] = (
            (x - mean) * scale * extra[k, 0:1, :].astype(F32)
        ).astype(BF)
    projected = jnp.dot(out_ref[...], weights[...], preferred_element_type=F32)
    attend(projected.astype(BF), weights.shape[1] // (3 * HEAD_DIM), attended_ref)


def fill_and_norm(part, order, keep, ids, own, near, late, weights, encs, shares):
    tokens, width = own.shape
    cols = len(encs)
    vis = encs[0].shape[0]
    whole = lambda a: pl.BlockSpec(a.shape, lambda i, *_: (0, 0))
    row = lambda i, *_: (i, 0)
    return pl.pallas_call(
        functools.partial(norm_kernel, cols, part, len(late)),
        out_shape=[
            jax.ShapeDtypeStruct((tokens, cols * width), BF),
            jax.ShapeDtypeStruct((tokens, weights.shape[1] // 3), BF),
        ],
        grid_spec=pltpu.PrefetchScalarGridSpec(
            num_scalar_prefetch=1,
            grid=(tokens // L,),
            in_specs=[whole(keep)]
            + [pl.BlockSpec((L, p.shape[1]), row) for p in (ids, own, near)]
            + [whole(a) for a in late + [weights] + encs + shares],
            out_specs=[
                pl.BlockSpec((L, cols * width), row),
                pl.BlockSpec((L, weights.shape[1] // 3), row),
            ],
            scratch_shapes=[
                pltpu.VMEM((cols, 16, width), BF),
                pltpu.VMEM((cols, cols * vis + 128 + len(late) * part, width), BF),
                pltpu.VMEM((cols, L, width), BF),
            ],
        ),
        compiler_params=pltpu.CompilerParams(vmem_limit_bytes=50 * MIB),
        cost_estimate=LIGHT,
        name="fill_norm",
    )(order, keep, ids, own, near, *late, weights, *encs, *shares)


def heads_kernel(heads, source_ref, x_ref, *refs):
    weights, out_ref = refs[:-1], refs[-1]
    if len(weights) == 1:
        acc = jnp.dot(x_ref[...], weights[0][...], preferred_element_type=F32)
    else:
        acc = None
        for p, w_ref in enumerate(weights):
            block = w_ref.shape[0]
            low = pl.multiple_of(source_ref[p] * block, block)
            term = jnp.dot(x_ref[:, pl.ds(low, block)], w_ref[...], preferred_element_type=F32)
            acc = term if acc is None else acc + term
    attend(acc.astype(BF), heads, out_ref)


def some_heads(source, normed, weights, heads):
    tokens, depth = normed.shape
    hw = heads * HEAD_DIM
    return pl.pallas_call(
        functools.partial(heads_kernel, heads),
        out_shape=jax.ShapeDtypeStruct((tokens, hw), BF),
        grid_spec=pltpu.PrefetchScalarGridSpec(
            num_scalar_prefetch=1,
            grid=(tokens // L,),
            in_specs=[pl.BlockSpec((L, depth), lambda i, *_: (i, 0))]
            + [pl.BlockSpec(w.shape, lambda i, *_: (0, 0)) for w in weights],
            out_specs=pl.BlockSpec((L, hw), lambda i, *_: (i, 0)),
        ),
        compiler_params=pltpu.CompilerParams(vmem_limit_bytes=VMEM),
        cost_estimate=LIGHT,
        name=f"heads_{heads}",
    )(source, normed, *weights)


def out_kernel(n, has_acc, at_ref, *refs):
    xs, ws = refs[:n], refs[n : 2 * n]
    out_ref = refs[-1]
    acc = refs[2 * n][...] if has_acc else None
    for x_ref, w_ref in zip(xs, ws):
        term = jnp.dot(x_ref[...], w_ref[...], preferred_element_type=F32)
        acc = term if acc is None else acc + term
    out_ref[...] = acc.astype(out_ref.dtype)


def project(order, groups, weight, acc, last):
    tokens = next(iter(groups[0][1].values())).shape[0]
    width = weight.shape[1]
    row = lambda i, *_: (i, 0)
    xs, x_specs, w_specs = [], [], []
    for first, parts in groups:
        depth = parts[min(parts)].shape[1]
        for k, x in sorted(parts.items()):
            xs.append(x)
            x_specs.append(pl.BlockSpec((L, depth), row))
            w_specs.append(
                pl.BlockSpec(
                    (depth, width),
                    lambda i, at, k=k, first=first, depth=depth: (
                        at[k] * (width // depth) + first // depth, 0
                    ),
                )
            )
    n = len(xs)
    operands = xs + [weight] * n
    specs = x_specs + w_specs
    alias = {}
    if acc is not None:
        specs.append(pl.BlockSpec((L, width), row))
        operands.append(acc)
        if not last:
            alias = {1 + 2 * n: 0}
    depths = sum(x.shape[1] for x in xs)
    return pl.pallas_call(
        functools.partial(out_kernel, n, acc is not None),
        out_shape=jax.ShapeDtypeStruct((tokens, width), BF if last else F32),
        grid_spec=pltpu.PrefetchScalarGridSpec(
            num_scalar_prefetch=1,
            grid=(tokens // L,),
            in_specs=specs,
            out_specs=pl.BlockSpec((L, width), row),
        ),
        input_output_aliases=alias,
        compiler_params=pltpu.CompilerParams(vmem_limit_bytes=40 * MIB),
        cost_estimate=LIGHT,
        name="out_proj",
    )(order, *operands)


def head_chunks(heads):
    return [(low, 2) for low in range(0, heads, 2)]


def gate(*trees):
    return lax.optimization_barrier(trees)


def on_device(
    rows, cols, enc_out, keep, pos_ids, mask_token, pos_table, gain, w_query, w_key, w_value, w_out
):
    images = keep.shape[0]
    positions, width = pos_table.shape
    r, c = lax.axis_index("row"), lax.axis_index("col")
    order = (c - jnp.arange(cols, dtype=jnp.int32)) % cols
    chunks = head_chunks(width // HEAD_DIM)
    n = len(chunks)

    projections = (w_query, w_key, w_value)

    part = positions // rows
    owner, inner = pos_ids // part, pos_ids % part
    early = early_places(rows)
    later = [p for p in range(rows) if p not in early]

    offsets = row_offsets(rows)
    sources = [r ^ jnp.where(r % 2 == 1, odd, even) for even, odd in zip(offsets[0], offsets[1])]

    def ids_of(places):
        ids = inner - positions
        for i, p in enumerate(places):
            ids = ids + jnp.where(owner == sources[p], positions + i * part, 0)
        return ids.reshape(images * L, 1)

    lane = lax.broadcasted_iota(jnp.int32, (images * L, 128), 1)
    own_ids = pos_ids.reshape(images * L, 1)
    ids = jnp.where(lane == 0, own_ids, jnp.where(lane == 1, ids_of(early), ids_of(later)))

    small = (
        ids,
        (keep + L * jnp.arange(images, dtype=jnp.int32)[:, None]).reshape(cols, -1)[order].reshape(1, -1),
        jnp.stack(sources).astype(jnp.int32),
        order,
    )

    share = lax.dynamic_slice_in_dim(pos_table, r * part, part, axis=0)
    pad = jnp.zeros((14, width), BF)
    share = jnp.concatenate([share, gain[None], mask_token[None], pad], axis=0)
    others = range(1, cols)

    gather = lambda w: lax.all_gather(w, "row", axis=0, tiled=True)
    split = rows == 8 and n >= 4
    weights = [[gather(pack(projections, chunks[:1])[0])]]
    shares = [share] + [shift(share, cols, k) for k in others]
    packs = list(pack(projections, chunks[1:]))
    placed_own = place(ids, 0, [pos_table])
    shares, placed_own, enc, packs, w_out, small = gate(
        shares, placed_own, enc_out, packs, w_out, small
    )
    ids, numbers, source, order = small

    weights += [[gather(p)] for p in (packs[:-1] if split else packs)]
    w_full = gather(w_out)
    late = Rows(packs[-1], rows)

    table = Rows(jnp.concatenate([shares[k][:part] for k in others], axis=1), rows)
    encs = near_cols(enc, cols)
    table.start()
    table.parts, encs = gate(table.parts, encs)

    encs = far_cols(encs, cols)
    table.forward()
    placed = place(ids, 1, table.blocks(early))
    table.parts, encs, placed = gate(table.parts, encs, placed)

    table.finish()
    if split:
        late.fetch(1, 2)
    normed, attended = fill_and_norm(
        part, order, numbers, ids, placed_own, placed, table.blocks(later), weights[0][0], encs, shares
    )
    attended, normed, late.parts = gate(attended, normed, late.parts)

    sent, half = [], None
    for k in range(1, n):
        whole = far_cols(half, cols) if half else None
        half = near_cols(attended, cols)
        if split and k == 1:
            late.fetch(3, 5)
        if split and k == 2:
            late.fetch(4, 6, 7)
        if split and k == n - 1:
            weights.append(late.blocks(range(rows)))
        attended = some_heads(source, normed, weights[k], chunks[k][1])
        attended, normed, half, whole, late.parts = gate(attended, normed, half, whole, late.parts)
        if whole:
            sent.append(whole)
    group = lambda k: (chunks[k][0] * HEAD_DIM, dict(enumerate(sent[k])))
    whole = far_cols(half, cols)
    half = near_cols(attended, cols)
    acc = None
    if n > 2:
        acc = project(order, [group(k) for k in range(n - 2)], w_full, None, False)
    half, whole, acc = gate(half, whole, acc)
    sent.append(whole)
    first = chunks[n - 1][0] * HEAD_DIM
    here = {k: x for k, x in enumerate(half) if x is not None}
    acc = project(order, [group(n - 2), (first, here)], w_full, acc, False)
    far = {k: x for k, x in enumerate(far_cols(half, cols)) if k not in here}
    return project(order, [(first, far)], w_full, acc, True)


def solution(mesh):
    rows, cols = mesh.shape["row"], mesh.shape["col"]
    in_specs = (
        P(("row", "col"), None),
        P("row", None),
        P("row", None),
        P("col"),
        P(None, "col"),
        P("col"),
        P("row", "col"),
        P("row", "col"),
        P("row", "col"),
        P("row", "col"),
    )
    return jax.shard_map(
        functools.partial(on_device, rows, cols),
        mesh=mesh,
        in_specs=in_specs,
        out_specs=P("row", "col"),
        check_vma=False,
    )
```

```python
import functools

import jax
import jax.numpy as jnp
import numpy as np
from jax import lax
from jax.experimental import pallas as pl
from jax.experimental.pallas import tpu as pltpu
from jax.sharding import PartitionSpec as P

L = 256
HEAD_DIM = 128
EPS = 1e-05
BF = jnp.bfloat16
F32 = jnp.float32
MIB = 1 << 20
VMEM = 60 * MIB
LIGHT = pl.CostEstimate(flops=1, bytes_accessed=1, transcendentals=0)


def after(x, *deps):
    return lax.optimization_barrier((x,) + deps)[0]


def row_offsets(rows):
    if rows == 8:
        even, odd = [0, 2, 4, 6, 1, 5, 3, 7], [0, 4, 2, 6, 1, 3, 5, 7]
        return [odd if r % 2 else even for r in range(rows)]
    offsets, bit = [0], rows // 2
    while bit:
        offsets = offsets + [t ^ bit for t in offsets]
        bit //= 2
    return [offsets] * rows


def swap(x, pairs):
    return lax.ppermute(x, "row", pairs)


class Rows:
    def __init__(self, x, rows):
        self.rows, self.x = rows, x
        self.parts = {0: x}
        self.first = [(r, r ^ (4 if r % 2 else 2)) for r in range(rows)]
        self.second = [(r, r ^ (2 if r % 2 else 4)) for r in range(rows)]
        self.sibling = [(r, r ^ 1) for r in range(rows)]

    def fetch(self, *places):
        for p in places:
            pairs = {1: self.first, 2: self.second, 3: self.second}.get(p, self.sibling)
            origin = {1: 0, 2: 0, 3: 1}.get(p, p - 4)
            self.parts[p] = swap(self.parts[origin], pairs)

    def start(self):
        if self.rows == 8:
            self.fetch(1, 2, 4)
            return
        blocks, bit = [self.x], self.rows // 2
        while bit:
            pairs = [(r, r ^ bit) for r in range(self.rows)]
            blocks = blocks + [swap(t, pairs) for t in blocks]
            bit //= 2
        self.parts = dict(enumerate(blocks))

    def forward(self):
        if self.rows == 8:
            self.fetch(3, 5, 6)

    def finish(self):
        if self.rows == 8:
            self.fetch(7)

    def blocks(self, places):
        return [self.parts[p] for p in places]


def early_places(rows):
    return [0, 1, 2, 4, 5, 6] if rows == 8 else list(range(rows // 2))


def shift(x, cols, step):
    return lax.ppermute(x, "col", [(c, (c + step) % cols) for c in range(cols)])


def near_cols(x, cols):
    blocks = [x] + [None] * (cols - 1)
    blocks[1] = shift(x, cols, 1)
    if cols > 2:
        blocks[cols - 1] = shift(x, cols, -1)
    return blocks


def far_cols(blocks, cols):
    blocks = list(blocks)
    for k in range(2, cols // 2 + 1):
        if blocks[k] is None:
            blocks[k] = shift(blocks[k - 1], cols, 1)
    for k in range(cols - 2, cols // 2, -1):
        blocks[k] = shift(blocks[k + 1], cols, -1)
    return blocks


def col_gather(x, cols):
    return far_cols(near_cols(x, cols), cols)


def pack_kernel(count, *refs):
    for k in range(len(refs) // (count + 1)):
        out_ref = refs[len(refs) * count // (count + 1) + k]
        width = out_ref.shape[1] // count
        for j in range(count):
            out_ref[:, j * width : (j + 1) * width] = refs[k * count + j][...]


def pack(weights, chunks):
    depth = weights[0].shape[0]
    in_specs, out_specs, shapes = [], [], []
    for low, size in chunks:
        width = size * HEAD_DIM
        spec = pl.BlockSpec((depth, width), lambda i, at=low // size: (0, at))
        in_specs += [spec] * len(weights)
        wide = (depth, width * len(weights))
        out_specs.append(pl.BlockSpec(wide, lambda i: (0, 0)))
        shapes.append(jax.ShapeDtypeStruct(wide, BF))
    return pl.pallas_call(
        functools.partial(pack_kernel, len(weights)),
        out_shape=shapes,
        grid=(1,),
        in_specs=in_specs,
        out_specs=out_specs,
        compiler_params=pltpu.CompilerParams(vmem_limit_bytes=VMEM),
        cost_estimate=LIGHT,
        name="pack",
    )(*(list(weights) * len(chunks)))


def attend(projected, heads, out_ref):
    hw = heads * HEAD_DIM
    scale = HEAD_DIM**-0.5
    cut = lambda j, h: projected[:, j * hw + h * HEAD_DIM : j * hw + (h + 1) * HEAD_DIM]
    scores = [
        lax.dot_general(
            cut(0, h), cut(1, h), (((1,), (1,)), ((), ())), preferred_element_type=F32
        ) * scale
        for h in range(heads)
    ]
    raised = [jnp.exp(s - jnp.max(s, axis=1, keepdims=True)) for s in scores]
    probs = [(e * (1.0 / jnp.sum(e, axis=1, keepdims=True))).astype(BF) for e in raised]
    out = [jnp.dot(p, cut(2, h), preferred_element_type=F32) for h, p in enumerate(probs)]
    out_ref[...] = jnp.concatenate(out, axis=1).astype(BF)


def place_kernel(parts, column_of_ids, ids_ref, *refs):
    tables, out_ref, held = refs[: sum(parts)], refs[-2], refs[-1]
    width = out_ref.shape[1]

    @pl.when(pl.program_id(0) == 0)
    def _():
        column, at = 0, 0
        for count in parts:
            low = 0
            for block in tables[at : at + count]:
                held[low : low + block.shape[0], column : column + block.shape[1]] = block[...]
                low += block.shape[0]
            at += count
            column += block.shape[1]

    wide = lax.broadcasted_iota(jnp.int32, (L, held.shape[0]), 1)
    ids = ids_ref[:, column_of_ids : column_of_ids + 1]
    pick = jnp.where(wide == ids, 1.0, 0.0).astype(BF)
    step = min(width, 1024)
    for low in range(0, width, step):
        out_ref[:, low : low + step] = jnp.dot(
            pick, held[:, low : low + step], preferred_element_type=F32
        ).astype(BF)


def place(ids, which, *tables):
    tokens = ids.shape[0]
    positions = sum(t.shape[0] for t in tables[0])
    width = sum(t[0].shape[1] for t in tables)
    operands = [t for table in tables for t in table]
    return pl.pallas_call(
        functools.partial(place_kernel, [len(t) for t in tables], which),
        out_shape=jax.ShapeDtypeStruct((tokens, width), BF),
        grid=(tokens // L,),
        in_specs=[pl.BlockSpec((L, ids.shape[1]), lambda i: (i, 0))]
        + [pl.BlockSpec(t.shape, lambda i: (0, 0)) for t in operands],
        out_specs=pl.BlockSpec((L, width), lambda i: (i, 0)),
        scratch_shapes=[pltpu.VMEM((positions, width), BF)],
        compiler_params=pltpu.CompilerParams(vmem_limit_bytes=VMEM),
        cost_estimate=LIGHT,
        name="place",
    )(ids, *operands)


def norm_kernel(cols, part, n_late, col_ref, keep_ref, ids_ref, own_ref, near_ref, *refs):
    late, weights, refs = refs[:n_late], refs[n_late], refs[n_late + 1 :]
    encs, shares = refs[:cols], refs[cols : 2 * cols]
    out_ref, attended_ref, extra, table, held = refs[2 * cols :]
    image = pl.program_id(0)
    width = held.shape[2]
    vis = encs[0].shape[0]
    seen_all = cols * vis
    base = seen_all + 128

    @pl.when(image == 0)
    def _():
        for k in range(cols):
            both = shares[k][part : part + 16, :]
            extra[k] = both
            at = col_ref[k]
            table[at, seen_all : seen_all + 16, :] = both
            table[at, seen_all + 16 : base, :] = jnp.zeros((112, width), BF)
            for z in range(cols):
                table[z, k * vis : (k + 1) * vis, :] = encs[k][:, z * width : (z + 1) * width]
            if k:
                for p in range(n_late):
                    low = base + p * part
                    table[at, low : low + part, :] = late[p][:, (k - 1) * width : k * width]

    here = lax.broadcasted_iota(jnp.int32, (L, seen_all), 0) + image * L
    seen = jnp.where(here == keep_ref[...], 1.0, 0.0)
    hidden = 1.0 - jnp.max(seen, axis=1, keepdims=True)
    lane = lax.broadcasted_iota(jnp.int32, (L, 128), 1)
    wide = lax.broadcasted_iota(jnp.int32, (L, n_late * part), 1)
    rest = jnp.where(wide == ids_ref[:, 2:3], 1.0, 0.0)
    pick = jnp.concatenate([seen, jnp.where(lane == 1, hidden, 0.0), rest], axis=1).astype(BF)
    def filled(k):
        at = col_ref[k]
        if k == 0:
            return jnp.dot(pick[:, :base], table[at, :base, :], preferred_element_type=F32)
        return jnp.dot(pick, table[at], preferred_element_type=F32)

    squares = jnp.zeros((L, 1), F32)
    total = jnp.zeros((L, 1), F32)
    products = [filled(0)]
    for k in range(cols):
        if k + 1 < cols:
            products.append(filled(k + 1))
        placed = own_ref[...] if k == 0 else near_ref[:, (k - 1) * width : k * width]
        xb = (products[k] + placed.astype(F32)).astype(BF)
        held[k] = xb
        x = xb.astype(F32)
        total = total + jnp.sum(x, axis=1, keepdims=True)
        squares = squares + jnp.sum(x * x, axis=1, keepdims=True)
    mean = total / (cols * width)
    var = squares / (cols * width) - mean * mean
    scale = lax.rsqrt(var + EPS)
    for k in range(cols):
        x = held[k].astype(F32)
        low = pl.multiple_of(col_ref[k] * width, width)
        out_ref[:, pl.ds(low, width)] = (
            (x - mean) * scale * extra[k, 0:1, :].astype(F32)
        ).astype(BF)
    projected = jnp.dot(out_ref[...], weights[...], preferred_element_type=F32)
    attend(projected.astype(BF), weights.shape[1] // (3 * HEAD_DIM), attended_ref)


def fill_and_norm(part, order, keep, ids, own, near, late, weights, encs, shares):
    tokens, width = own.shape
    cols = len(encs)
    vis = encs[0].shape[0]
    whole = lambda a: pl.BlockSpec(a.shape, lambda i, *_: (0, 0))
    row = lambda i, *_: (i, 0)
    return pl.pallas_call(
        functools.partial(norm_kernel, cols, part, len(late)),
        out_shape=[
            jax.ShapeDtypeStruct((tokens, cols * width), BF),
            jax.ShapeDtypeStruct((tokens, weights.shape[1] // 3), BF),
        ],
        grid_spec=pltpu.PrefetchScalarGridSpec(
            num_scalar_prefetch=1,
            grid=(tokens // L,),
            in_specs=[whole(keep)]
            + [pl.BlockSpec((L, p.shape[1]), row) for p in (ids, own, near)]
            + [whole(a) for a in late + [weights] + encs + shares],
            out_specs=[
                pl.BlockSpec((L, cols * width), row),
                pl.BlockSpec((L, weights.shape[1] // 3), row),
            ],
            scratch_shapes=[
                pltpu.VMEM((cols, 16, width), BF),
                pltpu.VMEM((cols, cols * vis + 128 + len(late) * part, width), BF),
                pltpu.VMEM((cols, L, width), BF),
            ],
        ),
        compiler_params=pltpu.CompilerParams(vmem_limit_bytes=50 * MIB),
        cost_estimate=LIGHT,
        name="fill_norm",
    )(order, keep, ids, own, near, *late, weights, *encs, *shares)


def heads_kernel(heads, source_ref, x_ref, *refs):
    weights, out_ref = refs[:-1], refs[-1]
    if len(weights) == 1:
        acc = jnp.dot(x_ref[...], weights[0][...], preferred_element_type=F32)
    else:
        acc = None
        for p, w_ref in enumerate(weights):
            block = w_ref.shape[0]
            low = pl.multiple_of(source_ref[p] * block, block)
            term = jnp.dot(x_ref[:, pl.ds(low, block)], w_ref[...], preferred_element_type=F32)
            acc = term if acc is None else acc + term
    attend(acc.astype(BF), heads, out_ref)


def some_heads(source, normed, weights, heads):
    tokens, depth = normed.shape
    hw = heads * HEAD_DIM
    return pl.pallas_call(
        functools.partial(heads_kernel, heads),
        out_shape=jax.ShapeDtypeStruct((tokens, hw), BF),
        grid_spec=pltpu.PrefetchScalarGridSpec(
            num_scalar_prefetch=1,
            grid=(tokens // L,),
            in_specs=[pl.BlockSpec((L, depth), lambda i, *_: (i, 0))]
            + [pl.BlockSpec(w.shape, lambda i, *_: (0, 0)) for w in weights],
            out_specs=pl.BlockSpec((L, hw), lambda i, *_: (i, 0)),
        ),
        compiler_params=pltpu.CompilerParams(vmem_limit_bytes=VMEM),
        cost_estimate=LIGHT,
        name=f"heads_{heads}",
    )(source, normed, *weights)


def out_kernel(n, has_acc, at_ref, *refs):
    xs, ws = refs[:n], refs[n : 2 * n]
    out_ref = refs[-1]
    acc = refs[2 * n][...] if has_acc else None
    for x_ref, w_ref in zip(xs, ws):
        term = jnp.dot(x_ref[...], w_ref[...], preferred_element_type=F32)
        acc = term if acc is None else acc + term
    out_ref[...] = acc.astype(out_ref.dtype)


def project(order, groups, weight, acc, last):
    tokens = next(iter(groups[0][1].values())).shape[0]
    width = weight.shape[1]
    row = lambda i, *_: (i, 0)
    xs, x_specs, w_specs = [], [], []
    for first, parts in groups:
        depth = parts[min(parts)].shape[1]
        for k, x in sorted(parts.items()):
            xs.append(x)
            x_specs.append(pl.BlockSpec((L, depth), row))
            w_specs.append(
                pl.BlockSpec(
                    (depth, width),
                    lambda i, at, k=k, first=first, depth=depth: (
                        at[k] * (width // depth) + first // depth, 0
                    ),
                )
            )
    n = len(xs)
    operands = xs + [weight] * n
    specs = x_specs + w_specs
    alias = {}
    if acc is not None:
        specs.append(pl.BlockSpec((L, width), row))
        operands.append(acc)
        if not last:
            alias = {1 + 2 * n: 0}
    depths = sum(x.shape[1] for x in xs)
    return pl.pallas_call(
        functools.partial(out_kernel, n, acc is not None),
        out_shape=jax.ShapeDtypeStruct((tokens, width), BF if last else F32),
        grid_spec=pltpu.PrefetchScalarGridSpec(
            num_scalar_prefetch=1,
            grid=(tokens // L,),
            in_specs=specs,
            out_specs=pl.BlockSpec((L, width), row),
        ),
        input_output_aliases=alias,
        compiler_params=pltpu.CompilerParams(vmem_limit_bytes=40 * MIB),
        cost_estimate=LIGHT,
        name="out_proj",
    )(order, *operands)


def head_chunks(heads):
    return [(low, 2) for low in range(0, heads, 2)]


def gate(*trees):
    return lax.optimization_barrier(trees)


def on_device(
    rows, cols, enc_out, keep, pos_ids, mask_token, pos_table, gain, w_query, w_key, w_value, w_out
):
    images = keep.shape[0]
    positions, width = pos_table.shape
    r, c = lax.axis_index("row"), lax.axis_index("col")
    order = (c - jnp.arange(cols, dtype=jnp.int32)) % cols
    chunks = head_chunks(width // HEAD_DIM)
    n = len(chunks)

    projections = (w_query, w_key, w_value)

    part = positions // rows
    owner, inner = pos_ids // part, pos_ids % part
    early = early_places(rows)
    later = [p for p in range(rows) if p not in early]

    offsets = row_offsets(rows)
    sources = [r ^ jnp.where(r % 2 == 1, odd, even) for even, odd in zip(offsets[0], offsets[1])]

    def ids_of(places):
        ids = inner - positions
        for i, p in enumerate(places):
            ids = ids + jnp.where(owner == sources[p], positions + i * part, 0)
        return ids.reshape(images * L, 1)

    lane = lax.broadcasted_iota(jnp.int32, (images * L, 128), 1)
    own_ids = pos_ids.reshape(images * L, 1)
    ids = jnp.where(lane == 0, own_ids, jnp.where(lane == 1, ids_of(early), ids_of(later)))

    small = (
        ids,
        (keep + L * jnp.arange(images, dtype=jnp.int32)[:, None]).reshape(cols, -1)[order].reshape(1, -1),
        jnp.stack(sources).astype(jnp.int32),
        order,
    )

    share = lax.dynamic_slice_in_dim(pos_table, r * part, part, axis=0)
    pad = jnp.zeros((14, width), BF)
    share = jnp.concatenate([share, gain[None], mask_token[None], pad], axis=0)
    others = range(1, cols)

    gather = lambda w: lax.all_gather(w, "row", axis=0, tiled=True)
    turn = 2 if rows == 8 and n >= 4 else None
    weights = [[gather(pack(projections, chunks[:1])[0])]]
    shares = [share] + [shift(share, cols, k) for k in others]
    packs = list(pack(projections, chunks[1:]))
    placed_own = place(ids, 0, [pos_table])
    shares, placed_own, enc, packs, w_out, small = gate(
        shares, placed_own, enc_out, packs, w_out, small
    )
    ids, numbers, source, order = small

    weights += [[gather(p)] if k != turn else None for k, p in enumerate(packs, 1)]
    w_full = gather(w_out)
    late = Rows(packs[(turn or n - 1) - 1], rows)

    table = Rows(jnp.concatenate([shares[k][:part] for k in others], axis=1), rows)
    encs = near_cols(enc, cols)
    table.start()
    table.parts, encs = gate(table.parts, encs)

    encs = far_cols(encs, cols)
    table.forward()
    placed = place(ids, 1, table.blocks(early))
    table.parts, encs, placed = gate(table.parts, encs, placed)

    table.finish()
    if turn:
        late.fetch(1, 2)
    normed, attended = fill_and_norm(
        part, order, numbers, ids, placed_own, placed, table.blocks(later), weights[0][0], encs, shares
    )
    attended, normed, late.parts = gate(attended, normed, late.parts)

    sent, half = [], None
    for k in range(1, n):
        whole = far_cols(half, cols) if half else None
        half = near_cols(attended, cols)
        if turn and k == 1:
            late.fetch(3, 4, 5)
        if turn and k == 2:
            late.fetch(6, 7)
            weights[k] = late.blocks(range(rows))
        attended = some_heads(source, normed, weights[k], chunks[k][1])
        attended, normed, half, whole, late.parts = gate(attended, normed, half, whole, late.parts)
        if whole:
            sent.append(whole)
    group = lambda k: (chunks[k][0] * HEAD_DIM, dict(enumerate(sent[k])))
    whole = far_cols(half, cols)
    half = near_cols(attended, cols)
    acc = None
    if n > 2:
        acc = project(order, [group(k) for k in range(n - 2)], w_full, None, False)
    half, whole, acc = gate(half, whole, acc)
    sent.append(whole)
    first = chunks[n - 1][0] * HEAD_DIM
    here = {k: x for k, x in enumerate(half) if x is not None}
    acc = project(order, [group(n - 2), (first, here)], w_full, acc, False)
    far = {k: x for k, x in enumerate(far_cols(half, cols)) if k not in here}
    return project(order, [(first, far)], w_full, acc, True)


def solution(mesh):
    rows, cols = mesh.shape["row"], mesh.shape["col"]
    in_specs = (
        P(("row", "col"), None),
        P("row", None),
        P("row", None),
        P("col"),
        P(None, "col"),
        P("col"),
        P("row", "col"),
        P("row", "col"),
        P("row", "col"),
        P("row", "col"),
    )
    return jax.shard_map(
        functools.partial(on_device, rows, cols),
        mesh=mesh,
        in_specs=in_specs,
        out_specs=P("row", "col"),
        check_vma=False,
    )
```

```python
import functools

import jax
import jax.numpy as jnp
import numpy as np
from jax import lax
from jax.experimental import pallas as pl
from jax.experimental.pallas import tpu as pltpu
from jax.sharding import PartitionSpec as P

L = 256
HEAD_DIM = 128
EPS = 1e-05
BF = jnp.bfloat16
F32 = jnp.float32
MIB = 1 << 20
VMEM = 60 * MIB
LIGHT = pl.CostEstimate(flops=1, bytes_accessed=1, transcendentals=0)


def after(x, *deps):
    return lax.optimization_barrier((x,) + deps)[0]


def row_offsets(rows):
    if rows == 8:
        even, odd = [0, 2, 4, 6, 1, 5, 3, 7], [0, 4, 2, 6, 1, 3, 5, 7]
        return [odd if r % 2 else even for r in range(rows)]
    offsets, bit = [0], rows // 2
    while bit:
        offsets = offsets + [t ^ bit for t in offsets]
        bit //= 2
    return [offsets] * rows


def swap(x, pairs):
    return lax.ppermute(x, "row", pairs)


class Rows:
    def __init__(self, x, rows):
        self.rows, self.x = rows, x
        self.parts = {0: x}
        self.first = [(r, r ^ (4 if r % 2 else 2)) for r in range(rows)]
        self.second = [(r, r ^ (2 if r % 2 else 4)) for r in range(rows)]
        self.sibling = [(r, r ^ 1) for r in range(rows)]

    def fetch(self, *places):
        for p in places:
            pairs = {1: self.first, 2: self.second, 3: self.second}.get(p, self.sibling)
            origin = {1: 0, 2: 0, 3: 1}.get(p, p - 4)
            self.parts[p] = swap(self.parts[origin], pairs)

    def start(self):
        if self.rows == 8:
            self.fetch(1, 2, 4)
            return
        blocks, bit = [self.x], self.rows // 2
        while bit:
            pairs = [(r, r ^ bit) for r in range(self.rows)]
            blocks = blocks + [swap(t, pairs) for t in blocks]
            bit //= 2
        self.parts = dict(enumerate(blocks))

    def forward(self):
        if self.rows == 8:
            self.fetch(3, 5, 6)

    def finish(self):
        if self.rows == 8:
            self.fetch(7)

    def blocks(self, places):
        return [self.parts[p] for p in places]


def early_places(rows):
    return [0, 1, 2, 4, 5, 6] if rows == 8 else list(range(rows // 2))


def shift(x, cols, step):
    return lax.ppermute(x, "col", [(c, (c + step) % cols) for c in range(cols)])


def near_cols(x, cols):
    blocks = [x] + [None] * (cols - 1)
    blocks[1] = shift(x, cols, 1)
    if cols > 2:
        blocks[cols - 1] = shift(x, cols, -1)
    return blocks


def far_cols(blocks, cols):
    blocks = list(blocks)
    for k in range(2, cols // 2 + 1):
        if blocks[k] is None:
            blocks[k] = shift(blocks[k - 1], cols, 1)
    for k in range(cols - 2, cols // 2, -1):
        blocks[k] = shift(blocks[k + 1], cols, -1)
    return blocks


def col_gather(x, cols):
    return far_cols(near_cols(x, cols), cols)


def pack_kernel(count, *refs):
    for k in range(len(refs) // (count + 1)):
        out_ref = refs[len(refs) * count // (count + 1) + k]
        width = out_ref.shape[1] // count
        for j in range(count):
            out_ref[:, j * width : (j + 1) * width] = refs[k * count + j][...]


def pack(weights, chunks):
    depth = weights[0].shape[0]
    in_specs, out_specs, shapes = [], [], []
    for low, size in chunks:
        width = size * HEAD_DIM
        spec = pl.BlockSpec((depth, width), lambda i, at=low // size: (0, at))
        in_specs += [spec] * len(weights)
        wide = (depth, width * len(weights))
        out_specs.append(pl.BlockSpec(wide, lambda i: (0, 0)))
        shapes.append(jax.ShapeDtypeStruct(wide, BF))
    return pl.pallas_call(
        functools.partial(pack_kernel, len(weights)),
        out_shape=shapes,
        grid=(1,),
        in_specs=in_specs,
        out_specs=out_specs,
        compiler_params=pltpu.CompilerParams(vmem_limit_bytes=VMEM),
        cost_estimate=LIGHT,
        name="pack",
    )(*(list(weights) * len(chunks)))


def attend(projected, heads, out_ref):
    hw = heads * HEAD_DIM
    scale = HEAD_DIM**-0.5
    cut = lambda j, h: projected[:, j * hw + h * HEAD_DIM : j * hw + (h + 1) * HEAD_DIM]
    scores = [
        lax.dot_general(
            cut(0, h), cut(1, h), (((1,), (1,)), ((), ())), preferred_element_type=F32
        ) * scale
        for h in range(heads)
    ]
    raised = [jnp.exp(s - jnp.max(s, axis=1, keepdims=True)) for s in scores]
    probs = [(e * (1.0 / jnp.sum(e, axis=1, keepdims=True))).astype(BF) for e in raised]
    out = [jnp.dot(p, cut(2, h), preferred_element_type=F32) for h, p in enumerate(probs)]
    out_ref[...] = jnp.concatenate(out, axis=1).astype(BF)


def place_kernel(parts, column_of_ids, ids_ref, *refs):
    tables, out_ref, held = refs[: sum(parts)], refs[-2], refs[-1]
    width = out_ref.shape[1]

    @pl.when(pl.program_id(0) == 0)
    def _():
        column, at = 0, 0
        for count in parts:
            low = 0
            for block in tables[at : at + count]:
                held[low : low + block.shape[0], column : column + block.shape[1]] = block[...]
                low += block.shape[0]
            at += count
            column += block.shape[1]

    wide = lax.broadcasted_iota(jnp.int32, (L, held.shape[0]), 1)
    ids = ids_ref[:, column_of_ids : column_of_ids + 1]
    pick = jnp.where(wide == ids, 1.0, 0.0).astype(BF)
    step = min(width, 1024)
    for low in range(0, width, step):
        out_ref[:, low : low + step] = jnp.dot(
            pick, held[:, low : low + step], preferred_element_type=F32
        ).astype(BF)


def place(ids, which, *tables):
    tokens = ids.shape[0]
    positions = sum(t.shape[0] for t in tables[0])
    width = sum(t[0].shape[1] for t in tables)
    operands = [t for table in tables for t in table]
    return pl.pallas_call(
        functools.partial(place_kernel, [len(t) for t in tables], which),
        out_shape=jax.ShapeDtypeStruct((tokens, width), BF),
        grid=(tokens // L,),
        in_specs=[pl.BlockSpec((L, ids.shape[1]), lambda i: (i, 0))]
        + [pl.BlockSpec(t.shape, lambda i: (0, 0)) for t in operands],
        out_specs=pl.BlockSpec((L, width), lambda i: (i, 0)),
        scratch_shapes=[pltpu.VMEM((positions, width), BF)],
        compiler_params=pltpu.CompilerParams(vmem_limit_bytes=VMEM),
        cost_estimate=LIGHT,
        name="place",
    )(ids, *operands)


def norm_kernel(cols, part, n_late, col_ref, keep_ref, ids_ref, own_ref, near_ref, *refs):
    late, weights, refs = refs[:n_late], refs[n_late], refs[n_late + 1 :]
    encs, shares = refs[:cols], refs[cols : 2 * cols]
    out_ref, attended_ref, extra, table, held = refs[2 * cols :]
    image = pl.program_id(0)
    width = held.shape[2]
    vis = encs[0].shape[0]
    seen_all = cols * vis
    base = seen_all + 128

    @pl.when(image == 0)
    def _():
        for k in range(cols):
            both = shares[k][part : part + 16, :]
            extra[k] = both
            at = col_ref[k]
            table[at, seen_all : seen_all + 16, :] = both
            table[at, seen_all + 16 : base, :] = jnp.zeros((112, width), BF)
            for z in range(cols):
                table[z, k * vis : (k + 1) * vis, :] = encs[k][:, z * width : (z + 1) * width]
            if k:
                for p in range(n_late):
                    low = base + p * part
                    table[at, low : low + part, :] = late[p][:, (k - 1) * width : k * width]

    here = lax.broadcasted_iota(jnp.int32, (L, seen_all), 0) + image * L
    seen = jnp.where(here == keep_ref[...], 1.0, 0.0)
    hidden = 1.0 - jnp.max(seen, axis=1, keepdims=True)
    lane = lax.broadcasted_iota(jnp.int32, (L, 128), 1)
    wide = lax.broadcasted_iota(jnp.int32, (L, n_late * part), 1)
    rest = jnp.where(wide == ids_ref[:, 2:3], 1.0, 0.0)
    pick = jnp.concatenate([seen, jnp.where(lane == 1, hidden, 0.0), rest], axis=1).astype(BF)
    def filled(k):
        at = col_ref[k]
        if k == 0:
            return jnp.dot(pick[:, :base], table[at, :base, :], preferred_element_type=F32)
        return jnp.dot(pick, table[at], preferred_element_type=F32)

    squares = jnp.zeros((L, 1), F32)
    total = jnp.zeros((L, 1), F32)
    products = [filled(0)]
    for k in range(cols):
        if k + 1 < cols:
            products.append(filled(k + 1))
        placed = own_ref[...] if k == 0 else near_ref[:, (k - 1) * width : k * width]
        xb = (products[k] + placed.astype(F32)).astype(BF)
        held[k] = xb
        x = xb.astype(F32)
        total = total + jnp.sum(x, axis=1, keepdims=True)
        squares = squares + jnp.sum(x * x, axis=1, keepdims=True)
    mean = total / (cols * width)
    var = squares / (cols * width) - mean * mean
    scale = lax.rsqrt(var + EPS)
    for k in range(cols):
        x = held[k].astype(F32)
        low = pl.multiple_of(col_ref[k] * width, width)
        out_ref[:, pl.ds(low, width)] = (
            (x - mean) * scale * extra[k, 0:1, :].astype(F32)
        ).astype(BF)
    projected = jnp.dot(out_ref[...], weights[...], preferred_element_type=F32)
    attend(projected.astype(BF), weights.shape[1] // (3 * HEAD_DIM), attended_ref)


def fill_and_norm(part, order, keep, ids, own, near, late, weights, encs, shares):
    tokens, width = own.shape
    cols = len(encs)
    vis = encs[0].shape[0]
    whole = lambda a: pl.BlockSpec(a.shape, lambda i, *_: (0, 0))
    row = lambda i, *_: (i, 0)
    return pl.pallas_call(
        functools.partial(norm_kernel, cols, part, len(late)),
        out_shape=[
            jax.ShapeDtypeStruct((tokens, cols * width), BF),
            jax.ShapeDtypeStruct((tokens, weights.shape[1] // 3), BF),
        ],
        grid_spec=pltpu.PrefetchScalarGridSpec(
            num_scalar_prefetch=1,
            grid=(tokens // L,),
            in_specs=[whole(keep)]
            + [pl.BlockSpec((L, p.shape[1]), row) for p in (ids, own, near)]
            + [whole(a) for a in late + [weights] + encs + shares],
            out_specs=[
                pl.BlockSpec((L, cols * width), row),
                pl.BlockSpec((L, weights.shape[1] // 3), row),
            ],
            scratch_shapes=[
                pltpu.VMEM((cols, 16, width), BF),
                pltpu.VMEM((cols, cols * vis + 128 + len(late) * part, width), BF),
                pltpu.VMEM((cols, L, width), BF),
            ],
        ),
        compiler_params=pltpu.CompilerParams(vmem_limit_bytes=50 * MIB),
        cost_estimate=LIGHT,
        name="fill_norm",
    )(order, keep, ids, own, near, *late, weights, *encs, *shares)


def heads_kernel(heads, source_ref, x_ref, *refs):
    weights, out_ref = refs[:-1], refs[-1]
    if len(weights) == 1:
        acc = jnp.dot(x_ref[...], weights[0][...], preferred_element_type=F32)
    else:
        acc = None
        for p, w_ref in enumerate(weights):
            block = w_ref.shape[0]
            low = pl.multiple_of(source_ref[p] * block, block)
            term = jnp.dot(x_ref[:, pl.ds(low, block)], w_ref[...], preferred_element_type=F32)
            acc = term if acc is None else acc + term
    attend(acc.astype(BF), heads, out_ref)


def some_heads(source, normed, weights, heads):
    tokens, depth = normed.shape
    hw = heads * HEAD_DIM
    return pl.pallas_call(
        functools.partial(heads_kernel, heads),
        out_shape=jax.ShapeDtypeStruct((tokens, hw), BF),
        grid_spec=pltpu.PrefetchScalarGridSpec(
            num_scalar_prefetch=1,
            grid=(tokens // L,),
            in_specs=[pl.BlockSpec((L, depth), lambda i, *_: (i, 0))]
            + [pl.BlockSpec(w.shape, lambda i, *_: (0, 0)) for w in weights],
            out_specs=pl.BlockSpec((L, hw), lambda i, *_: (i, 0)),
        ),
        compiler_params=pltpu.CompilerParams(vmem_limit_bytes=VMEM),
        cost_estimate=LIGHT,
        name=f"heads_{heads}",
    )(source, normed, *weights)


def out_kernel(n, has_acc, at_ref, *refs):
    xs, ws = refs[:n], refs[n : 2 * n]
    out_ref = refs[-1]
    acc = refs[2 * n][...] if has_acc else None
    for x_ref, w_ref in zip(xs, ws):
        term = jnp.dot(x_ref[...], w_ref[...], preferred_element_type=F32)
        acc = term if acc is None else acc + term
    out_ref[...] = acc.astype(out_ref.dtype)


def project(order, groups, weight, acc, last):
    tokens = next(iter(groups[0][1].values())).shape[0]
    width = weight.shape[1]
    row = lambda i, *_: (i, 0)
    xs, x_specs, w_specs = [], [], []
    for first, parts in groups:
        depth = parts[min(parts)].shape[1]
        for k, x in sorted(parts.items()):
            xs.append(x)
            x_specs.append(pl.BlockSpec((L, depth), row))
            w_specs.append(
                pl.BlockSpec(
                    (depth, width),
                    lambda i, at, k=k, first=first, depth=depth: (
                        at[k] * (width // depth) + first // depth, 0
                    ),
                )
            )
    n = len(xs)
    operands = xs + [weight] * n
    specs = x_specs + w_specs
    alias = {}
    if acc is not None:
        specs.append(pl.BlockSpec((L, width), row))
        operands.append(acc)
        if not last:
            alias = {1 + 2 * n: 0}
    depths = sum(x.shape[1] for x in xs)
    return pl.pallas_call(
        functools.partial(out_kernel, n, acc is not None),
        out_shape=jax.ShapeDtypeStruct((tokens, width), BF if last else F32),
        grid_spec=pltpu.PrefetchScalarGridSpec(
            num_scalar_prefetch=1,
            grid=(tokens // L,),
            in_specs=specs,
            out_specs=pl.BlockSpec((L, width), row),
        ),
        input_output_aliases=alias,
        compiler_params=pltpu.CompilerParams(vmem_limit_bytes=24 * MIB),
        cost_estimate=LIGHT,
        name="out_proj",
    )(order, *operands)


def head_chunks(heads):
    return [(low, 2) for low in range(0, heads, 2)]


def gate(*trees):
    return lax.optimization_barrier(trees)


def on_device(
    rows, cols, enc_out, keep, pos_ids, mask_token, pos_table, gain, w_query, w_key, w_value, w_out
):
    images = keep.shape[0]
    positions, width = pos_table.shape
    r, c = lax.axis_index("row"), lax.axis_index("col")
    order = (c - jnp.arange(cols, dtype=jnp.int32)) % cols
    chunks = head_chunks(width // HEAD_DIM)
    n = len(chunks)

    projections = (w_query, w_key, w_value)

    part = positions // rows
    owner, inner = pos_ids // part, pos_ids % part
    early = early_places(rows)
    later = [p for p in range(rows) if p not in early]

    offsets = row_offsets(rows)
    sources = [r ^ jnp.where(r % 2 == 1, odd, even) for even, odd in zip(offsets[0], offsets[1])]

    def ids_of(places):
        ids = inner - positions
        for i, p in enumerate(places):
            ids = ids + jnp.where(owner == sources[p], positions + i * part, 0)
        return ids.reshape(images * L, 1)

    lane = lax.broadcasted_iota(jnp.int32, (images * L, 128), 1)
    own_ids = pos_ids.reshape(images * L, 1)
    ids = jnp.where(lane == 0, own_ids, jnp.where(lane == 1, ids_of(early), ids_of(later)))

    small = (
        ids,
        (keep + L * jnp.arange(images, dtype=jnp.int32)[:, None]).reshape(cols, -1)[order].reshape(1, -1),
        jnp.stack(sources).astype(jnp.int32),
        order,
    )

    share = lax.dynamic_slice_in_dim(pos_table, r * part, part, axis=0)
    pad = jnp.zeros((14, width), BF)
    share = jnp.concatenate([share, gain[None], mask_token[None], pad], axis=0)
    others = range(1, cols)

    gather = lambda w: lax.all_gather(w, "row", axis=0, tiled=True)
    turn = 2 if rows == 8 and n >= 4 else None
    weights = [[gather(pack(projections, chunks[:1])[0])]]
    shares = [share] + [shift(share, cols, k) for k in others]
    packs = list(pack(projections, chunks[1:]))
    placed_own = place(ids, 0, [pos_table])
    shares, placed_own, enc, packs, w_out, small = gate(
        shares, placed_own, enc_out, packs, w_out, small
    )
    ids, numbers, source, order = small

    weights += [[gather(p)] if k != turn else None for k, p in enumerate(packs, 1)]
    w_full = gather(w_out)
    late = Rows(packs[(turn or n - 1) - 1], rows)

    table = Rows(jnp.concatenate([shares[k][:part] for k in others], axis=1), rows)
    encs = near_cols(enc, cols)
    table.start()
    table.parts, encs = gate(table.parts, encs)

    encs = far_cols(encs, cols)
    table.forward()
    placed = place(ids, 1, table.blocks(early))
    table.parts, encs, placed = gate(table.parts, encs, placed)

    table.finish()
    if turn:
        late.fetch(1, 2)
    normed, attended = fill_and_norm(
        part, order, numbers, ids, placed_own, placed, table.blocks(later), weights[0][0], encs, shares
    )
    attended, normed, late.parts = gate(attended, normed, late.parts)

    sent, half = [], None
    for k in range(1, n):
        whole = far_cols(half, cols) if half else None
        half = near_cols(attended, cols)
        if turn and k == 1:
            late.fetch(3, 4, 5)
        if turn and k == 2:
            late.fetch(6, 7)
            weights[k] = late.blocks(range(rows))
        attended = some_heads(source, normed, weights[k], chunks[k][1])
        attended, normed, half, whole, late.parts = gate(attended, normed, half, whole, late.parts)
        if whole:
            sent.append(whole)
    group = lambda k: (chunks[k][0] * HEAD_DIM, dict(enumerate(sent[k])))
    whole = far_cols(half, cols)
    half = near_cols(attended, cols)
    acc = None
    if n > 2:
        acc = project(order, [group(k) for k in range(n - 2)], w_full, None, False)
    half, whole, acc = gate(half, whole, acc)
    sent.append(whole)
    first = chunks[n - 1][0] * HEAD_DIM
    here = {k: x for k, x in enumerate(half) if x is not None}
    acc = project(order, [group(n - 2), (first, here)], w_full, acc, False)
    far = {k: x for k, x in enumerate(far_cols(half, cols)) if k not in here}
    return project(order, [(first, far)], w_full, acc, True)


def solution(mesh):
    rows, cols = mesh.shape["row"], mesh.shape["col"]
    in_specs = (
        P(("row", "col"), None),
        P("row", None),
        P("row", None),
        P("col"),
        P(None, "col"),
        P("col"),
        P("row", "col"),
        P("row", "col"),
        P("row", "col"),
        P("row", "col"),
    )
    return jax.shard_map(
        functools.partial(on_device, rows, cols),
        mesh=mesh,
        in_specs=in_specs,
        out_specs=P("row", "col"),
        check_vma=False,
    )
```

```python
import functools

import jax
import jax.numpy as jnp
import numpy as np
from jax import lax
from jax.experimental import pallas as pl
from jax.experimental.pallas import tpu as pltpu
from jax.sharding import PartitionSpec as P

L = 256
HEAD_DIM = 128
EPS = 1e-05
BF = jnp.bfloat16
F32 = jnp.float32
MIB = 1 << 20
VMEM = 60 * MIB
LIGHT = pl.CostEstimate(flops=1, bytes_accessed=1, transcendentals=0)


def after(x, *deps):
    return lax.optimization_barrier((x,) + deps)[0]


def row_offsets(rows):
    if rows == 8:
        even, odd = [0, 2, 4, 6, 1, 5, 3, 7], [0, 4, 2, 6, 1, 3, 5, 7]
        return [odd if r % 2 else even for r in range(rows)]
    offsets, bit = [0], rows // 2
    while bit:
        offsets = offsets + [t ^ bit for t in offsets]
        bit //= 2
    return [offsets] * rows


def swap(x, pairs):
    return lax.ppermute(x, "row", pairs)


class Rows:
    def __init__(self, x, rows):
        self.rows, self.x = rows, x
        self.parts = {0: x}
        self.first = [(r, r ^ (4 if r % 2 else 2)) for r in range(rows)]
        self.second = [(r, r ^ (2 if r % 2 else 4)) for r in range(rows)]
        self.sibling = [(r, r ^ 1) for r in range(rows)]

    def fetch(self, *places):
        for p in places:
            pairs = {1: self.first, 2: self.second, 3: self.second}.get(p, self.sibling)
            origin = {1: 0, 2: 0, 3: 1}.get(p, p - 4)
            self.parts[p] = swap(self.parts[origin], pairs)

    def start(self):
        if self.rows == 8:
            self.fetch(1, 2)
            return
        blocks, bit = [self.x], self.rows // 2
        while bit:
            pairs = [(r, r ^ bit) for r in range(self.rows)]
            blocks = blocks + [swap(t, pairs) for t in blocks]
            bit //= 2
        self.parts = dict(enumerate(blocks))

    def forward(self):
        if self.rows == 8:
            self.fetch(4, 5, 6, 3)

    def finish(self):
        if self.rows == 8:
            self.fetch(7)

    def blocks(self, places):
        return [self.parts[p] for p in places]


def early_places(rows):
    return [0, 1, 2, 4, 5, 6] if rows == 8 else list(range(rows // 2))


def shift(x, cols, step):
    return lax.ppermute(x, "col", [(c, (c + step) % cols) for c in range(cols)])


def near_cols(x, cols):
    blocks = [x] + [None] * (cols - 1)
    blocks[1] = shift(x, cols, 1)
    if cols > 2:
        blocks[cols - 1] = shift(x, cols, -1)
    return blocks


def far_cols(blocks, cols):
    blocks = list(blocks)
    for k in range(2, cols // 2 + 1):
        if blocks[k] is None:
            blocks[k] = shift(blocks[k - 1], cols, 1)
    for k in range(cols - 2, cols // 2, -1):
        blocks[k] = shift(blocks[k + 1], cols, -1)
    return blocks


def col_gather(x, cols):
    return far_cols(near_cols(x, cols), cols)


def pack_kernel(count, *refs):
    for k in range(len(refs) // (count + 1)):
        out_ref = refs[len(refs) * count // (count + 1) + k]
        width = out_ref.shape[1] // count
        for j in range(count):
            out_ref[:, j * width : (j + 1) * width] = refs[k * count + j][...]


def pack(weights, chunks):
    depth = weights[0].shape[0]
    in_specs, out_specs, shapes = [], [], []
    for low, size in chunks:
        width = size * HEAD_DIM
        spec = pl.BlockSpec((depth, width), lambda i, at=low // size: (0, at))
        in_specs += [spec] * len(weights)
        wide = (depth, width * len(weights))
        out_specs.append(pl.BlockSpec(wide, lambda i: (0, 0)))
        shapes.append(jax.ShapeDtypeStruct(wide, BF))
    return pl.pallas_call(
        functools.partial(pack_kernel, len(weights)),
        out_shape=shapes,
        grid=(1,),
        in_specs=in_specs,
        out_specs=out_specs,
        compiler_params=pltpu.CompilerParams(vmem_limit_bytes=VMEM),
        cost_estimate=LIGHT,
        name="pack",
    )(*(list(weights) * len(chunks)))


def attend(projected, heads, out_ref):
    hw = heads * HEAD_DIM
    scale = HEAD_DIM**-0.5
    cut = lambda j, h: projected[:, j * hw + h * HEAD_DIM : j * hw + (h + 1) * HEAD_DIM]
    scores = [
        lax.dot_general(
            cut(0, h), cut(1, h), (((1,), (1,)), ((), ())), preferred_element_type=F32
        ) * scale
        for h in range(heads)
    ]
    raised = [jnp.exp(s - jnp.max(s, axis=1, keepdims=True)) for s in scores]
    probs = [(e * (1.0 / jnp.sum(e, axis=1, keepdims=True))).astype(BF) for e in raised]
    out = [jnp.dot(p, cut(2, h), preferred_element_type=F32) for h, p in enumerate(probs)]
    out_ref[...] = jnp.concatenate(out, axis=1).astype(BF)


def place_kernel(parts, column_of_ids, ids_ref, *refs):
    tables, out_ref, held = refs[: sum(parts)], refs[-2], refs[-1]
    width = out_ref.shape[1]

    @pl.when(pl.program_id(0) == 0)
    def _():
        column, at = 0, 0
        for count in parts:
            low = 0
            for block in tables[at : at + count]:
                held[low : low + block.shape[0], column : column + block.shape[1]] = block[...]
                low += block.shape[0]
            at += count
            column += block.shape[1]

    wide = lax.broadcasted_iota(jnp.int32, (L, held.shape[0]), 1)
    ids = ids_ref[:, column_of_ids : column_of_ids + 1]
    pick = jnp.where(wide == ids, 1.0, 0.0).astype(BF)
    step = min(width, 1024)
    for low in range(0, width, step):
        out_ref[:, low : low + step] = jnp.dot(
            pick, held[:, low : low + step], preferred_element_type=F32
        ).astype(BF)


def place(ids, which, *tables):
    tokens = ids.shape[0]
    positions = sum(t.shape[0] for t in tables[0])
    width = sum(t[0].shape[1] for t in tables)
    operands = [t for table in tables for t in table]
    return pl.pallas_call(
        functools.partial(place_kernel, [len(t) for t in tables], which),
        out_shape=jax.ShapeDtypeStruct((tokens, width), BF),
        grid=(tokens // L,),
        in_specs=[pl.BlockSpec((L, ids.shape[1]), lambda i: (i, 0))]
        + [pl.BlockSpec(t.shape, lambda i: (0, 0)) for t in operands],
        out_specs=pl.BlockSpec((L, width), lambda i: (i, 0)),
        scratch_shapes=[pltpu.VMEM((positions, width), BF)],
        compiler_params=pltpu.CompilerParams(vmem_limit_bytes=VMEM),
        cost_estimate=LIGHT,
        name="place",
    )(ids, *operands)


def norm_kernel(cols, part, n_late, col_ref, keep_ref, ids_ref, own_ref, near_ref, *refs):
    late, weights, refs = refs[:n_late], refs[n_late], refs[n_late + 1 :]
    encs, shares = refs[:cols], refs[cols : 2 * cols]
    out_ref, attended_ref, extra, table, held = refs[2 * cols :]
    image = pl.program_id(0)
    width = held.shape[2]
    vis = encs[0].shape[0]
    seen_all = cols * vis
    base = seen_all + 128

    @pl.when(image == 0)
    def _():
        for k in range(cols):
            both = shares[k][part : part + 16, :]
            extra[k] = both
            at = col_ref[k]
            table[at, seen_all : seen_all + 16, :] = both
            table[at, seen_all + 16 : base, :] = jnp.zeros((112, width), BF)
            for z in range(cols):
                table[z, k * vis : (k + 1) * vis, :] = encs[k][:, z * width : (z + 1) * width]
            if k:
                for p in range(n_late):
                    low = base + p * part
                    table[at, low : low + part, :] = late[p][:, (k - 1) * width : k * width]

    here = lax.broadcasted_iota(jnp.int32, (L, seen_all), 0) + image * L
    seen = jnp.where(here == keep_ref[...], 1.0, 0.0)
    hidden = 1.0 - jnp.max(seen, axis=1, keepdims=True)
    lane = lax.broadcasted_iota(jnp.int32, (L, 128), 1)
    wide = lax.broadcasted_iota(jnp.int32, (L, n_late * part), 1)
    rest = jnp.where(wide == ids_ref[:, 2:3], 1.0, 0.0)
    pick = jnp.concatenate([seen, jnp.where(lane == 1, hidden, 0.0), rest], axis=1).astype(BF)
    def filled(k):
        at = col_ref[k]
        if k == 0:
            return jnp.dot(pick[:, :base], table[at, :base, :], preferred_element_type=F32)
        return jnp.dot(pick, table[at], preferred_element_type=F32)

    squares = jnp.zeros((L, 1), F32)
    total = jnp.zeros((L, 1), F32)
    products = [filled(0)]
    for k in range(cols):
        if k + 1 < cols:
            products.append(filled(k + 1))
        placed = own_ref[...] if k == 0 else near_ref[:, (k - 1) * width : k * width]
        xb = (products[k] + placed.astype(F32)).astype(BF)
        held[k] = xb
        x = xb.astype(F32)
        total = total + jnp.sum(x, axis=1, keepdims=True)
        squares = squares + jnp.sum(x * x, axis=1, keepdims=True)
    mean = total / (cols * width)
    var = squares / (cols * width) - mean * mean
    scale = lax.rsqrt(var + EPS)
    for k in range(cols):
        x = held[k].astype(F32)
        low = pl.multiple_of(col_ref[k] * width, width)
        out_ref[:, pl.ds(low, width)] = (
            (x - mean) * scale * extra[k, 0:1, :].astype(F32)
        ).astype(BF)
    projected = jnp.dot(out_ref[...], weights[...], preferred_element_type=F32)
    attend(projected.astype(BF), weights.shape[1] // (3 * HEAD_DIM), attended_ref)


def fill_and_norm(part, order, keep, ids, own, near, late, weights, encs, shares):
    tokens, width = own.shape
    cols = len(encs)
    vis = encs[0].shape[0]
    whole = lambda a: pl.BlockSpec(a.shape, lambda i, *_: (0, 0))
    row = lambda i, *_: (i, 0)
    return pl.pallas_call(
        functools.partial(norm_kernel, cols, part, len(late)),
        out_shape=[
            jax.ShapeDtypeStruct((tokens, cols * width), BF),
            jax.ShapeDtypeStruct((tokens, weights.shape[1] // 3), BF),
        ],
        grid_spec=pltpu.PrefetchScalarGridSpec(
            num_scalar_prefetch=1,
            grid=(tokens // L,),
            in_specs=[whole(keep)]
            + [pl.BlockSpec((L, p.shape[1]), row) for p in (ids, own, near)]
            + [whole(a) for a in late + [weights] + encs + shares],
            out_specs=[
                pl.BlockSpec((L, cols * width), row),
                pl.BlockSpec((L, weights.shape[1] // 3), row),
            ],
            scratch_shapes=[
                pltpu.VMEM((cols, 16, width), BF),
                pltpu.VMEM((cols, cols * vis + 128 + len(late) * part, width), BF),
                pltpu.VMEM((cols, L, width), BF),
            ],
        ),
        compiler_params=pltpu.CompilerParams(vmem_limit_bytes=50 * MIB),
        cost_estimate=LIGHT,
        name="fill_norm",
    )(order, keep, ids, own, near, *late, weights, *encs, *shares)


def heads_kernel(heads, source_ref, x_ref, *refs):
    weights, out_ref = refs[:-1], refs[-1]
    if len(weights) == 1:
        acc = jnp.dot(x_ref[...], weights[0][...], preferred_element_type=F32)
    else:
        acc = None
        for p, w_ref in enumerate(weights):
            block = w_ref.shape[0]
            low = pl.multiple_of(source_ref[p] * block, block)
            term = jnp.dot(x_ref[:, pl.ds(low, block)], w_ref[...], preferred_element_type=F32)
            acc = term if acc is None else acc + term
    attend(acc.astype(BF), heads, out_ref)


def some_heads(source, normed, weights, heads):
    tokens, depth = normed.shape
    hw = heads * HEAD_DIM
    return pl.pallas_call(
        functools.partial(heads_kernel, heads),
        out_shape=jax.ShapeDtypeStruct((tokens, hw), BF),
        grid_spec=pltpu.PrefetchScalarGridSpec(
            num_scalar_prefetch=1,
            grid=(tokens // L,),
            in_specs=[pl.BlockSpec((L, depth), lambda i, *_: (i, 0))]
            + [pl.BlockSpec(w.shape, lambda i, *_: (0, 0)) for w in weights],
            out_specs=pl.BlockSpec((L, hw), lambda i, *_: (i, 0)),
        ),
        compiler_params=pltpu.CompilerParams(vmem_limit_bytes=VMEM),
        cost_estimate=LIGHT,
        name=f"heads_{heads}",
    )(source, normed, *weights)


def out_kernel(n, has_acc, at_ref, *refs):
    xs, ws = refs[:n], refs[n : 2 * n]
    out_ref = refs[-1]
    acc = refs[2 * n][...] if has_acc else None
    for x_ref, w_ref in zip(xs, ws):
        term = jnp.dot(x_ref[...], w_ref[...], preferred_element_type=F32)
        acc = term if acc is None else acc + term
    out_ref[...] = acc.astype(out_ref.dtype)


def project(order, groups, weight, acc, last):
    tokens = next(iter(groups[0][1].values())).shape[0]
    width = weight.shape[1]
    row = lambda i, *_: (i, 0)
    xs, x_specs, w_specs = [], [], []
    for first, parts in groups:
        depth = parts[min(parts)].shape[1]
        for k, x in sorted(parts.items()):
            xs.append(x)
            x_specs.append(pl.BlockSpec((L, depth), row))
            w_specs.append(
                pl.BlockSpec(
                    (depth, width),
                    lambda i, at, k=k, first=first, depth=depth: (
                        at[k] * (width // depth) + first // depth, 0
                    ),
                )
            )
    n = len(xs)
    operands = xs + [weight] * n
    specs = x_specs + w_specs
    alias = {}
    if acc is not None:
        specs.append(pl.BlockSpec((L, width), row))
        operands.append(acc)
        if not last:
            alias = {1 + 2 * n: 0}
    depths = sum(x.shape[1] for x in xs)
    return pl.pallas_call(
        functools.partial(out_kernel, n, acc is not None),
        out_shape=jax.ShapeDtypeStruct((tokens, width), BF if last else F32),
        grid_spec=pltpu.PrefetchScalarGridSpec(
            num_scalar_prefetch=1,
            grid=(tokens // L,),
            in_specs=specs,
            out_specs=pl.BlockSpec((L, width), row),
        ),
        input_output_aliases=alias,
        compiler_params=pltpu.CompilerParams(vmem_limit_bytes=24 * MIB),
        cost_estimate=LIGHT,
        name="out_proj",
    )(order, *operands)


def head_chunks(heads):
    return [(low, 2) for low in range(0, heads, 2)]


def gate(*trees):
    return lax.optimization_barrier(trees)


def on_device(
    rows, cols, enc_out, keep, pos_ids, mask_token, pos_table, gain, w_query, w_key, w_value, w_out
):
    images = keep.shape[0]
    positions, width = pos_table.shape
    r, c = lax.axis_index("row"), lax.axis_index("col")
    order = (c - jnp.arange(cols, dtype=jnp.int32)) % cols
    chunks = head_chunks(width // HEAD_DIM)
    n = len(chunks)

    projections = (w_query, w_key, w_value)

    part = positions // rows
    owner, inner = pos_ids // part, pos_ids % part
    early = early_places(rows)
    later = [p for p in range(rows) if p not in early]

    offsets = row_offsets(rows)
    sources = [r ^ jnp.where(r % 2 == 1, odd, even) for even, odd in zip(offsets[0], offsets[1])]

    def ids_of(places):
        ids = inner - positions
        for i, p in enumerate(places):
            ids = ids + jnp.where(owner == sources[p], positions + i * part, 0)
        return ids.reshape(images * L, 1)

    lane = lax.broadcasted_iota(jnp.int32, (images * L, 128), 1)
    own_ids = pos_ids.reshape(images * L, 1)
    ids = jnp.where(lane == 0, own_ids, jnp.where(lane == 1, ids_of(early), ids_of(later)))

    small = (
        ids,
        (keep + L * jnp.arange(images, dtype=jnp.int32)[:, None]).reshape(cols, -1)[order].reshape(1, -1),
        jnp.stack(sources).astype(jnp.int32),
        order,
    )

    share = lax.dynamic_slice_in_dim(pos_table, r * part, part, axis=0)
    pad = jnp.zeros((14, width), BF)
    share = jnp.concatenate([share, gain[None], mask_token[None], pad], axis=0)
    others = range(1, cols)

    gather = lambda w: lax.all_gather(w, "row", axis=0, tiled=True)
    turn = 2 if rows == 8 and n >= 4 else None
    weights = [[gather(pack(projections, chunks[:1])[0])]]
    shares = [share] + [shift(share, cols, k) for k in others]
    packs = list(pack(projections, chunks[1:]))
    placed_own = place(ids, 0, [pos_table])
    shares, placed_own, enc, packs, w_out, small = gate(
        shares, placed_own, enc_out, packs, w_out, small
    )
    ids, numbers, source, order = small

    weights += [[gather(p)] if k != turn else None for k, p in enumerate(packs, 1)]
    w_full = gather(w_out)
    late = Rows(packs[(turn or n - 1) - 1], rows)

    table = Rows(jnp.concatenate([shares[k][:part] for k in others], axis=1), rows)
    encs = near_cols(enc, cols)
    table.start()
    table.parts, encs = gate(table.parts, encs)

    encs = far_cols(encs, cols)
    table.forward()
    placed = place(ids, 1, table.blocks(early))
    table.parts, encs, placed = gate(table.parts, encs, placed)

    table.finish()
    if turn:
        late.fetch(1, 2)
    normed, attended = fill_and_norm(
        part, order, numbers, ids, placed_own, placed, table.blocks(later), weights[0][0], encs, shares
    )
    attended, normed, late.parts = gate(attended, normed, late.parts)

    sent, half = [], None
    for k in range(1, n):
        whole = far_cols(half, cols) if half else None
        half = near_cols(attended, cols)
        if turn and k == 1:
            late.fetch(3, 4, 5)
        if turn and k == 2:
            late.fetch(6, 7)
            weights[k] = late.blocks(range(rows))
        attended = some_heads(source, normed, weights[k], chunks[k][1])
        attended, normed, half, whole, late.parts = gate(attended, normed, half, whole, late.parts)
        if whole:
            sent.append(whole)
    group = lambda k: (chunks[k][0] * HEAD_DIM, dict(enumerate(sent[k])))
    whole = far_cols(half, cols)
    half = near_cols(attended, cols)
    acc = None
    if n > 2:
        acc = project(order, [group(k) for k in range(n - 2)], w_full, None, False)
    half, whole, acc = gate(half, whole, acc)
    sent.append(whole)
    first = chunks[n - 1][0] * HEAD_DIM
    here = {k: x for k, x in enumerate(half) if x is not None}
    acc = project(order, [group(n - 2), (first, here)], w_full, acc, False)
    far = {k: x for k, x in enumerate(far_cols(half, cols)) if k not in here}
    return project(order, [(first, far)], w_full, acc, True)


def solution(mesh):
    rows, cols = mesh.shape["row"], mesh.shape["col"]
    in_specs = (
        P(("row", "col"), None),
        P("row", None),
        P("row", None),
        P("col"),
        P(None, "col"),
        P("col"),
        P("row", "col"),
        P("row", "col"),
        P("row", "col"),
        P("row", "col"),
    )
    return jax.shard_map(
        functools.partial(on_device, rows, cols),
        mesh=mesh,
        in_specs=in_specs,
        out_specs=P("row", "col"),
        check_vma=False,
    )
```
